128 devices in a mesh: dp: 8 (over z, core), shard: 16 (over y, x).
Axes of the slice: x: 4, y: 4, z: 4, core: 2. Of those that a mesh axis runs over, the one named last changes fastest.
Arguments:
- grad_parts: float32 [8, 2048, 8192], P('dp', 'shard'), may hold values from -0.3125 to 0.3125
- moment: float32 [16, 128, 8192], P('shard', 'dp'), may hold values from -0.75 to 0.75
- second: float32 [16, 128, 8192], P('shard', 'dp'), may hold values from 0.001 to 0.01
- left_prev: float32 [8, 16, 1, 512, 512], P('dp', 'shard'), may hold values from -1 to 5, as said below
- right_prev: float32 [8, 16, 1, 512, 512], P('dp', 'shard'), may hold values from -1 to 5, as said below
- owners: int32 [64], replicated, may hold values from 0 to 15, as said below
- newton_steps: int32 [64], replicated, may hold values from 2 to 3
Outputs:
- update: float32 [16, 128, 8192], P('shard', 'dp')
- new_moment: float32 [16, 128, 8192], P('shard', 'dp')
- new_second: float32 [16, 128, 8192], P('shard', 'dp')
- new_left: float32 [8, 16, 1, 512, 512], P('dp', 'shard')
- new_right: float32 [8, 16, 1, 512, 512], P('dp', 'shard')
- root_left: float32 [8, 16, 1, 512, 512], P('dp', 'shard')
- root_right: float32 [8, 16, 1, 512, 512], P('dp', 'shard')
The draws below stay inside these ranges and needn't reach their ends.
Inputs may be any that keep to these rules, and one draw needn't show every extreme that they name: `owners`: among the 16 blocks of any block-row at most 2 share an owner, and one shard index owns exactly 2 blocks in every block-row. `left_prev`: each slot is a symmetric positive definite matrix. `right_prev`: each slot is a symmetric positive definite matrix.
All inputs are finite; a program needn't handle non-finite values.
Results may differ from the reference program's by a relative error of at most 0.00018.
Values sent between devices are 32-bit elements; how exact they have to be, the bound alone decides.
A program may use at most 64 MiB of HBM per device.

```python
import math
import jax
import jax.numpy as jnp
from jax import lax

D = 8192
B = 512
CAP = 2
MAXN = 3
RT = 2048
NBR = 4
NBC = 16
NB = 64
SR = 128
SLOTS = 1
N_DP = 8
N_SHARD = 16


def definite_slots(key, lowest, highest):
    jitter_key, diagonal_key = jax.random.split(key)
    jitter = jax.random.uniform(jitter_key, (N_DP, N_SHARD, SLOTS, B, B), jnp.float32, -1.4, 1.4) / B
    symmetric = 0.5 * (jitter + jnp.swapaxes(jitter, -1, -2))
    diagonal = jax.random.uniform(diagonal_key, (N_DP, N_SHARD, SLOTS, B), jnp.float32, lowest, highest)
    identity = jnp.eye(B, dtype=jnp.float32)
    return symmetric * (1.0 - identity) + diagonal[..., :, None] * identity


def draw_left_prev(key, part):
    key = jax.random.fold_in(key, 3)
    return definite_slots(key, 1.5, 2.5)


def draw_right_prev(key, part):
    key = jax.random.fold_in(key, 5)
    return definite_slots(key, 1.5, 2.5)


def draw_owners(key, part):
    key = jax.random.fold_in(key, 7)
    pick_key, row_key = jax.random.split(key)
    favored = jax.random.randint(pick_key, (), 0, N_SHARD)
    places = N_SHARD * CAP

    def one_row(single_key):
        ranking_key, column_key = jax.random.split(single_key)
        ranking = jax.random.permutation(ranking_key, places)
        holder = jnp.arange(places) // CAP
        scores = jnp.where(holder == favored, ranking - places, ranking)
        chosen = jnp.argsort(scores)[:NBC]
        chosen_owner = chosen // CAP
        columns = jax.random.permutation(column_key, NBC)
        return chosen_owner[jnp.argsort(columns)]
    row_owners = jax.vmap(one_row)(jax.random.split(row_key, NBR))
    return row_owners.reshape(NB).astype(jnp.int32)


def draw_newton_steps(key, part):
    key = jax.random.fold_in(key, 13)
    count_key, marked_key = jax.random.split(key)
    counts = jax.random.randint(count_key, (NB,), 2, MAXN + 1)
    marked = jax.random.randint(marked_key, (), 0, NB)
    return jnp.where(jnp.arange(NB) == marked, MAXN, counts).astype(jnp.int32)


def block_levels(rng, dims, cuts, smallest, top_value):
    def one(dim, parts):
        heights = jax.random.uniform(jax.random.fold_in(jax.random.fold_in(rng, 6), dim), (parts,), jnp.float32, smallest / len(cuts), top_value / len(cuts))
        return jnp.repeat(jnp.exp(heights), dims[dim] // parts).reshape((-1,) + (1,) * (len(dims) - dim - 1))

    loudness = one(*cuts[0])
    for cut in cuts[1:]:
        loudness = loudness * one(*cut)
    return loudness


def centred(stream_key, dims, deviation, limit, pieces=(), kind=jnp.bfloat16):
    result = jax.random.normal(stream_key, dims, jnp.float32) * deviation
    if len(pieces) > 0:
        result = block_levels(stream_key, dims, pieces, -0.22, 0.18) * result
    return jnp.clip(result, min=-limit, max=limit).astype(kind)


def setup_inputs(seed: int = 0) -> dict:
    streams_of = jax.random.split(jax.random.key(seed), 8)
    return {
        "grad_parts": centred(streams_of[0], (N_DP, RT, D), 0.02, 0.3125, ((0, 8), (1, 16)), jnp.float32),
        "moment": centred(streams_of[1], (N_SHARD, SR, D), 0.05, 0.75, ((0, 16), (1, 8)), jnp.float32),
        "second": jnp.clip(jnp.exp(math.log(0.01) - 2.30258502 * jax.random.uniform(streams_of[2], (N_SHARD, SR, D), jnp.float32) ** block_levels(streams_of[2], (N_SHARD, SR, D), ((0, 16), (1, 8)), -0.2, 0.2)), 0.001, 0.01),
        "left_prev": draw_left_prev(jax.random.fold_in(streams_of[7], 71), 0),
        "right_prev": draw_right_prev(jax.random.fold_in(streams_of[7], 71), 0),
        "owners": draw_owners(jax.random.fold_in(streams_of[7], 71), 0),
        "newton_steps": draw_newton_steps(jax.random.fold_in(streams_of[7], 71), 0),
    }


def matmul(first, second_factor):
    return jnp.dot(first, second_factor, precision=lax.Precision.HIGHEST)

def inverse_root(statistic, step_count):
    identity = jnp.eye(statistic.shape[0], dtype=statistic.dtype)
    shifted = statistic + 0.0001 * identity
    scaling = 2.5 / jnp.sqrt(jnp.sum(shifted * shifted))
    scaled = scaling * shifted
    inverse = jnp.sqrt(jnp.sqrt(scaling)) * identity

    def advance(position, state_pair):
        current, matrix = state_pair
        factor = 1.25 * identity - 0.25 * matrix
        square = matmul(factor, factor)
        return (matmul(current, factor), matmul(square, matmul(square, matrix)))
    inverse, scaled = lax.fori_loop(0, step_count - 1, advance, (inverse, scaled))
    return matmul(inverse, 1.25 * identity - 0.25 * scaled)

def owner_places(owners, dp_count):
    block_ids = jnp.arange(owners.shape[0], dtype=jnp.int32)
    same_owner = owners[:, None] == owners[None, :]
    earlier = block_ids[None, :] < block_ids[:, None]
    ranking = lax.optimization_barrier(jnp.sum(same_owner & earlier, axis=1)).astype(jnp.int32)
    return (ranking % dp_count, ranking // dp_count)

def reference(grad_parts, moment, second, left_prev, right_prev, owners, newton_steps):
    gradient = lax.optimization_barrier(jnp.sum(grad_parts, axis=0))
    row_total, column_total = gradient.shape
    block_size = left_prev.shape[-1]
    row_blocks = row_total // block_size
    column_blocks = column_total // block_size
    first_old = moment.reshape(row_total, column_total)
    second_old = second.reshape(row_total, column_total)
    moment_next = 0.9 * first_old + 0.1 * gradient
    second_next = 0.99 * second_old + 0.01 * gradient * gradient
    adam = moment_next / (jnp.sqrt(second_next) + 1e-08)
    adam_sq = lax.optimization_barrier(jnp.sum((adam * adam).reshape(row_blocks, block_size, column_blocks, block_size), axis=(1, 3))).reshape(-1)
    blocks = gradient.reshape(row_blocks, block_size, column_blocks, block_size).transpose(0, 2, 1, 3)
    blocks = blocks.reshape(row_blocks * column_blocks, block_size, block_size)
    dest_dp, slot_of = owner_places(owners, N_DP)
    left_old = left_prev[dest_dp, owners, slot_of]
    right_old = right_prev[dest_dp, owners, slot_of]

    def one_block(operands):
        block, left_before, right_before, step_count, square_sum = operands
        left_stat = 0.95 * left_before + matmul(block, block.T)
        right_stat = 0.95 * right_before + matmul(block.T, block)
        left_root = inverse_root(left_stat, step_count)
        right_root = inverse_root(right_stat, step_count)
        direction = matmul(matmul(left_root, block), right_root)
        update_block = direction * (jnp.sqrt(square_sum) / jnp.sqrt(jnp.sum(direction * direction) + 1e-12))
        return (left_stat, right_stat, left_root, right_root, update_block)
    results = lax.map(one_block, (blocks, left_old, right_old, newton_steps, adam_sq))

    def to_slots(values):
        return jnp.zeros(left_prev.shape, jnp.float32).at[dest_dp, owners, slot_of].set(values)
    update_full = results[4].reshape(row_blocks, column_blocks, block_size, block_size).transpose(0, 2, 1, 3)
    update_full = update_full.reshape(moment.shape)
    return (update_full, moment_next.reshape(moment.shape), second_next.reshape(moment.shape), to_slots(results[0]), to_slots(results[1]), to_slots(results[2]), to_slots(results[3]))
```

```python
import functools

import jax
import jax.numpy as jnp
from jax import lax
from jax.experimental import pallas as pl
from jax.experimental.pallas import tpu as pltpu
from jax.sharding import PartitionSpec as P

MESH = pl.DeviceIdType.MESH
CORES = 2
SUB = 8
CAP = 2
MIB = 1 << 20


def routes(owners, newton_steps, my_dp, my_shard, dims):
    ndp, nshard, nx, nbr, nbc = dims
    ids = jnp.arange(nbr * nbc, dtype=jnp.int32)
    row = ids // nbc
    earlier = (owners[:, None] == owners[None, :]) & (ids[None, :] < ids[:, None])
    rank = jnp.sum(earlier, axis=1, dtype=jnp.int32)
    sub = jnp.sum(earlier & (row[None, :] == row[:, None]), axis=1, dtype=jnp.int32)
    my_row = my_shard // nx

    def pick(count, key, chosen, value):
        hit = (jnp.arange(count, dtype=jnp.int32)[:, None] == key[None, :]) & chosen[None, :]
        return jnp.sum(jnp.where(hit, value[None, :], 0), axis=1, dtype=jnp.int32)

    mine = owners == my_shard
    here = row == my_row
    slot = owners * CAP + sub
    column = ids % nbc
    always = jnp.full_like(ids, 1)
    sends = pick(nshard * CAP, slot, here, column)
    by_rank = pick(ndp, rank, mine, row * CAP + sub)
    by_row = pick(nbr * CAP, row * CAP + sub, mine, rank)
    finals = pick(nbc, column, here, slot)
    place = mine & (rank == my_dp)
    steps = jnp.sum(jnp.where(place, newton_steps, 0), keepdims=True)
    taken = jnp.sum(jnp.where(place, always, 0), keepdims=True)
    return jnp.concatenate([sends, by_rank, by_row, finals, steps, taken]).astype(jnp.int32)


def offsets(dims):
    ndp, nshard, nx, nbr, nbc = dims
    sends = 0
    by_rank = sends + nshard * CAP
    by_row = by_rank + ndp
    finals = by_row + nbr * CAP
    steps = finals + nbc
    return sends, by_rank, by_row, finals, steps


def greet(peers):
    barrier = pltpu.get_barrier_semaphore()
    for peer in peers:
        pl.semaphore_signal(barrier, inc=1, device_id=peer, device_id_type=MESH)
    pl.semaphore_wait(barrier, len(peers))


def forward_kernel(dims, block, chunks, tab, grad, mom, sec,
                   gblk, mom_out, sec_out, adam_out,
                   loc, pair, first_up, first_down, from_below, from_above,
                   gsel, mbuf, vbuf, send1, recv1, send2, asend, arecv, xsend, xrecv,
                   loc_sem, pair_s, pair_r, ring_s, ring_r, p1_s, p1_r, p2_s, p2_r,
                   a_s, a_r, x_s, x_r, io_sem):
    ndp, nshard, nx, nbr, nbc = dims
    o_sends, o_rank, _, _, _ = offsets(dims)
    nz = ndp // CORES
    columns = nbc * block
    half = columns // 2
    rows_dev = SUB * chunks
    me_d = lax.axis_index("dp")
    me_s = lax.axis_index("shard")
    z = me_d // CORES
    core = me_d % CORES
    my_x = me_s % nx
    my_row = me_s // nx

    def zed(step):
        return (z + step) % nz

    def rows_of(zz, cc, h):
        return pl.ds(pl.multiple_of((zz * CORES + cc) * rows_dev + h * SUB, SUB), SUB)

    order = (2, 1, nz - 1, 0)
    loads = {}
    for h in range(chunks):
        for q, step in enumerate(order):
            loads[h, q] = pltpu.make_async_copy(
                grad.at[rows_of(zed(step), core, h), :], loc.at[h, q], loc_sem.at[h, q])
            loads[h, q].start()
    m_in = pltpu.make_async_copy(mom, mbuf, io_sem.at[0])
    v_in = pltpu.make_async_copy(sec, vbuf, io_sem.at[1])
    m_in.start()
    v_in.start()

    dps = [((me_d + k) % ndp, me_s) for k in range(1, ndp)]
    shards = [(me_d, (me_s + k) % nshard) for k in range(1, nshard)]
    greet(dps + shards)

    sibling = (z * CORES + (1 - core), me_s)
    above = (zed(1) * CORES + core, me_s)
    below = (zed(nz - 1) * CORES + core, me_s)
    pairs = {}
    for h in range(chunks):
        for q, step in enumerate(order):
            pairs[h, q] = pltpu.make_async_remote_copy(
                grad.at[rows_of(zed(step), 1 - core, h), :], pair.at[h, q],
                pair_s.at[h, q], pair_r.at[h, q], device_id=sibling, device_id_type=MESH)
            pairs[h, q].start()

    lo = pl.ds(0, half)
    hi = pl.ds(half, half)
    ring = {}

    def ring_send(h, index, src, dst, target):
        copy = pltpu.make_async_remote_copy(
            src, dst, ring_s.at[h, index], ring_r.at[h, index], device_id=target, device_id_type=MESH)
        copy.start()
        ring[h, index] = copy

    def merge(h, q):
        loads[h, q].wait()
        pairs[h, q].wait_recv()
        loc[h, q] = loc[h, q] + pair[h, q]

    def ring_one(h):
        merge(h, 0)
        ring_send(h, 0, loc.at[h, 0, :, lo], first_up.at[h], above)
        ring_send(h, 1, loc.at[h, 0, :, hi], first_down.at[h], below)
        merge(h, 1)
        ring_send(h, 2, loc.at[h, 1, :, hi], from_below.at[h, :, hi], above)
        merge(h, 2)
        ring_send(h, 3, loc.at[h, 2, :, lo], from_above.at[h, :, lo], below)
        merge(h, 3)

    def ring_two(h):
        ring[h, 0].wait_recv()
        loc[h, 1, :, lo] = loc[h, 1, :, lo] + first_up[h]
        ring_send(h, 4, loc.at[h, 1, :, lo], from_below.at[h, :, lo], above)
        ring[h, 1].wait_recv()
        loc[h, 2, :, hi] = loc[h, 2, :, hi] + first_down[h]
        ring_send(h, 5, loc.at[h, 2, :, hi], from_above.at[h, :, hi], below)

    def ring_end(h):
        for index in range(2, 6):
            ring[h, index].wait_recv()
        for c in range(nbc):
            cols = pl.ds(c * block, block)
            gsel[h, c] = (loc[h, 3, :, cols] + from_below[h, :, cols]) + from_above[h, :, cols]

    p1 = {}

    def exchange_shards(h):
        for k in range(1, nshard):
            target = (me_s + k) % nshard
            for j in range(CAP):
                send1[h, k, j] = gsel[h, tab[o_sends + target * CAP + j]]
            copy = pltpu.make_async_remote_copy(
                send1.at[h, k], recv1[h].at[me_s], p1_s.at[h, k], p1_r.at[h, k],
                device_id=(me_d, target), device_id_type=MESH)
            copy.start()
            p1[h, k] = copy
        for j in range(CAP):
            recv1[h][me_s, j] = gsel[h, tab[o_sends + me_s * CAP + j]]

    p2 = {}

    def exchange_dp(h):
        for k in range(1, nshard):
            p1[h, k].wait_recv()
        for k in list(range(1, ndp)) + [0]:
            target = (me_d + k) % ndp
            place = tab[o_rank + target]
            r = place // CAP
            j = place % CAP
            for x in range(nx):
                send2[h, k, x] = recv1[h][r * nx + x, j]
            if k:
                copy = pltpu.make_async_remote_copy(
                    send2.at[h, k], gblk.at[:, me_d, h], p2_s.at[h, k], p2_r.at[h, k],
                    device_id=(target, me_s), device_id_type=MESH)
            else:
                copy = pltpu.make_async_copy(send2.at[h, 0], gblk.at[:, me_d, h], p2_s.at[h, 0])
            copy.start()
            p2[h, k] = copy

    def adam_rows(h):
        rows = pl.ds(h * SUB, SUB)
        for c in range(nbc):
            cols = pl.ds(c * block, block)
            g = gsel[h, c]
            m = 0.9 * mbuf[rows, cols] + 0.1 * g
            v = 0.99 * vbuf[rows, cols] + 0.01 * g * g
            mbuf[rows, cols] = m
            vbuf[rows, cols] = v
            a = m / (jnp.sqrt(v) + 1e-08)
            sq = jnp.sum(a * a, axis=0, keepdims=True)
            part = sq[:, 0:128]
            for t in range(1, block // 128):
                part = part + sq[:, t * 128:(t + 1) * 128]
            if h == 0:
                asend[pl.ds(c, 1), :] = part
            else:
                asend[pl.ds(c, 1), :] = asend[pl.ds(c, 1), :] + part

    ring_one(0)
    ring_two(0)
    for h in range(1, chunks):
        ring_one(h)
    m_in.wait()
    v_in.wait()
    ring_end(0)
    exchange_shards(0)
    adam_rows(0)
    for h in range(1, chunks):
        ring_two(h)
        ring_end(h)
        exchange_shards(h)
        exchange_dp(h - 1)
        adam_rows(h)

    m_out = pltpu.make_async_copy(mbuf, mom_out, io_sem.at[0])
    v_out = pltpu.make_async_copy(vbuf, sec_out, io_sem.at[1])
    m_out.start()
    v_out.start()
    acopies = []
    for k in range(1, ndp):
        copy = pltpu.make_async_remote_copy(
            asend, arecv.at[k], a_s.at[k], a_r.at[k],
            device_id=((me_d + k) % ndp, me_s), device_id_type=MESH)
        copy.start()
        acopies.append(copy)
    exchange_dp(chunks - 1)
    total = asend[...]
    for k in range(1, ndp):
        acopies[k - 1].wait_recv()
        total = total + arecv[k]
    xsend[...] = total
    xcopies = []
    for k in range(1, nx):
        copy = pltpu.make_async_remote_copy(
            xsend, xrecv.at[k], x_s.at[k], x_r.at[k],
            device_id=(me_d, my_row * nx + (my_x + k) % nx), device_id_type=MESH)
        copy.start()
        xcopies.append(copy)
    for k in range(1, nx):
        xcopies[k - 1].wait_recv()
        total = total + xrecv[k]
    summed = jnp.sum(total, axis=1, keepdims=True)
    arecv[0] = jnp.broadcast_to(jnp.sqrt(summed), arecv.shape[1:])
    a_out = pltpu.make_async_copy(arecv.at[0], adam_out, io_sem.at[2])
    a_out.start()

    for h in range(chunks):
        for q in range(len(order)):
            pairs[h, q].wait_send()
        for index in range(6):
            ring[h, index].wait_send()
        for k in range(1, nshard):
            p1[h, k].wait_send()
        for k in range(1, ndp):
            p2[h, k].wait_send()
            p2[h, k].wait_recv()
        p2[h, 0].wait()
    for copy in acopies + xcopies:
        copy.wait_send()
    m_out.wait()
    v_out.wait()
    a_out.wait()


def forward(tab, grad, mom, sec, dims, block):
    ndp, nshard, nx, nbr, nbc = dims
    rows_dev, columns = mom.shape
    chunks = rows_dev // SUB
    half = columns // 2
    f32 = jnp.float32
    anywhere = pl.BlockSpec(memory_space=pl.ANY)
    dma = pltpu.SemaphoreType.DMA
    body = functools.partial(forward_kernel, dims, block, chunks)
    return pl.pallas_call(
        body,
        out_shape=(
            jax.ShapeDtypeStruct((nx, ndp, chunks, SUB, block), f32),
            jax.ShapeDtypeStruct((rows_dev, columns), f32),
            jax.ShapeDtypeStruct((rows_dev, columns), f32),
            jax.ShapeDtypeStruct((nbc, 128), f32),
        ),
        in_specs=[pl.BlockSpec(memory_space=pltpu.SMEM), anywhere, anywhere, anywhere],
        out_specs=(anywhere,) * 4,
        scratch_shapes=[
            pltpu.VMEM((chunks, 4, SUB, columns), f32),
            pltpu.VMEM((chunks, 4, SUB, columns), f32),
            pltpu.VMEM((chunks, SUB, half), f32),
            pltpu.VMEM((chunks, SUB, half), f32),
            pltpu.VMEM((chunks, SUB, columns), f32),
            pltpu.VMEM((chunks, SUB, columns), f32),
            pltpu.VMEM((chunks, nbc, SUB, block), f32),
            pltpu.VMEM((rows_dev, columns), f32),
            pltpu.VMEM((rows_dev, columns), f32),
            pltpu.VMEM((chunks, nshard, CAP, SUB, block), f32),
            [pltpu.VMEM((nshard, CAP, SUB, block), f32) for _ in range(chunks)],
            pltpu.VMEM((chunks, ndp, nx, SUB, block), f32),
            pltpu.VMEM((nbc, 128), f32),
            pltpu.VMEM((ndp, nbc, 128), f32),
            pltpu.VMEM((nbc, 128), f32),
            pltpu.VMEM((nx, nbc, 128), f32),
            dma((chunks, 4)),
            dma((chunks, 4)),
            dma((chunks, 4)),
            dma((chunks, 6)),
            dma((chunks, 6)),
            dma((chunks, nshard)),
            dma((chunks, nshard)),
            dma((chunks, ndp)),
            dma((chunks, ndp)),
            dma((ndp,)),
            dma((ndp,)),
            dma((nx,)),
            dma((nx,)),
            dma((3,)),
        ],
        compiler_params=pltpu.CompilerParams(
            collective_id=0, has_side_effects=True, vmem_limit_bytes=40 * MIB),
    )(tab, grad, mom, sec)


def split(value):
    high = value.astype(jnp.bfloat16)
    low = (value - high.astype(jnp.float32)).astype(jnp.bfloat16)
    return high, low


def product(first, second_factor, axes=((1,), (0,))):
    def dot(left, right):
        return lax.dot_general(left, right, (axes, ((), ())), preferred_element_type=jnp.float32)

    return dot(first[0], second_factor[0]) + (
        dot(first[0], second_factor[1]) + dot(first[1], second_factor[0]))


def owner_kernel(step_place, tab, gblk, left_prev, right_prev, mom, sec,
                 left_out, right_out, lroot_out, rroot_out, dir_out, mom_out, sec_out,
                 g_ref, stat, root, cur, sem):
    taken = tab[step_place + 1]
    m_copy = pltpu.make_async_copy(mom, mom_out, sem.at[0])
    v_copy = pltpu.make_async_copy(sec, sec_out, sem.at[1])
    m_copy.start()
    v_copy.start()
    size = g_ref.shape[0]
    outs = (left_out, right_out, lroot_out, rroot_out, dir_out)

    @pl.when(taken == 0)
    def _():
        stat[0] = jnp.zeros_like(stat[0])
        copies = [pltpu.make_async_copy(stat.at[0], out, sem.at[2 + i]) for i, out in enumerate(outs)]
        for copy in copies:
            copy.start()
        for copy in copies:
            copy.wait()

    @pl.when(taken != 0)
    def _():
        g_in = pltpu.make_async_copy(gblk, g_ref, sem.at[2])
        ins = [pltpu.make_async_copy(prev, stat.at[i], sem.at[3 + i])
               for i, prev in enumerate((left_prev, right_prev))]
        g_in.start()
        for copy in ins:
            copy.start()
        r_ids = lax.broadcasted_iota(jnp.int32, (size, size), 0)
        c_ids = lax.broadcasted_iota(jnp.int32, (size, size), 1)
        diagonal = r_ids == c_ids

        def complement(matrix):
            return jnp.where(diagonal, 1.25, 0.0) - 0.25 * matrix

        g_in.wait()
        g = split(g_ref[...])
        scales = []
        stat_outs = []
        for i, axes in enumerate((((1,), (1,)), ((0,), (0,)))):
            gram = product(g, g, axes)
            ins[i].wait()
            stat[i] = 0.95 * stat[i] + gram
            copy = pltpu.make_async_copy(stat.at[i], outs[i], sem.at[3 + i])
            copy.start()
            stat_outs.append(copy)
        for i in range(2):
            shifted = stat[i] + jnp.where(diagonal, 0.0001, 0.0)
            norm = jnp.sum(shifted * shifted)
            scale = 2.5 / jnp.sqrt(jnp.full((1, 1), norm))
            cur[i] = scale * shifted
            scales.append(jnp.sqrt(jnp.sqrt(scale)))

        def raise_four(factor, matrix):
            square = split(product(factor, factor))
            return product(square, split(product(square, matrix)))

        for i in range(2):
            matrix = cur[i]
            factor = split(complement(matrix))
            after = raise_four(factor, split(matrix))
            cur[i] = after
            root[i] = scales[i] * product(factor, split(complement(after)))

        @pl.when(tab[step_place] > 2)
        def _():
            for i in range(2):
                matrix = cur[i]
                after = raise_four(split(complement(matrix)), split(matrix))
                root[i] = product(split(root[i]), split(complement(after)))

        root_outs = []
        for i in range(2):
            copy = pltpu.make_async_copy(root.at[i], outs[2 + i], sem.at[5 + i])
            copy.start()
            root_outs.append(copy)
        for copy in stat_outs:
            copy.wait()
        way = product(split(product(split(root[0]), g)), split(root[1]))
        power = jnp.sum(way * way)
        g_ref[...] = way / jnp.sqrt(jnp.full((1, 1), power) + 1e-12)
        d_out = pltpu.make_async_copy(g_ref, dir_out, sem.at[2])
        d_out.start()
        for copy in root_outs:
            copy.wait()
        d_out.wait()

    m_copy.wait()
    v_copy.wait()


def owner_step(tab, gblk, left_prev, right_prev, mom, sec, step_place):
    size = gblk.shape[0]
    f32 = jnp.float32
    square = jax.ShapeDtypeStruct((size, size), f32)
    anywhere = pl.BlockSpec(memory_space=pl.ANY)
    return pl.pallas_call(
        functools.partial(owner_kernel, step_place),
        out_shape=(square,) * 5 + (jax.ShapeDtypeStruct(mom.shape, f32),) * 2,
        in_specs=[pl.BlockSpec(memory_space=pltpu.SMEM)] + [anywhere] * 5,
        out_specs=(anywhere,) * 7,
        scratch_shapes=[
            pltpu.VMEM((size, size), f32),
            pltpu.VMEM((2, size, size), f32),
            pltpu.VMEM((2, size, size), f32),
            pltpu.VMEM((2, size, size), f32),
            pltpu.SemaphoreType.DMA((7,)),
        ],
        compiler_params=pltpu.CompilerParams(vmem_limit_bytes=56 * MIB),
        cost_estimate=pl.CostEstimate(
            flops=120 * size ** 3, bytes_accessed=36 * size * size, transcendentals=0),
    )(tab, gblk, left_prev, right_prev, mom, sec)


def back_kernel(dims, block, chunks, tab, way, adam, update,
                recv2, send1, recv1, out, ad, p2_s, p2_r, p1_s, p1_r, io_sem):
    ndp, nshard, nx, nbr, nbc = dims
    _, _, o_row, o_final, _ = offsets(dims)
    me_d = lax.axis_index("dp")
    me_s = lax.axis_index("shard")
    a_in = pltpu.make_async_copy(adam, ad, io_sem.at[0])
    a_in.start()
    dps = [((me_d + k) % ndp, me_s) for k in range(1, ndp)]
    shards = [(me_d, (me_s + k) % nshard) for k in range(1, nshard)]
    greet(dps + shards)
    p2 = {}
    for h in range(chunks):
        for k in range(1, ndp):
            target = (me_d + k) % ndp
            copy = pltpu.make_async_remote_copy(
                way.at[:, target, h], recv2[h].at[me_d], p2_s.at[h, k], p2_r.at[h, k],
                device_id=(target, me_s), device_id_type=MESH)
            copy.start()
            p2[h, k] = copy
        copy = pltpu.make_async_copy(way.at[:, me_d, h], recv2[h].at[me_d], p2_s.at[h, 0])
        copy.start()
        p2[h, 0] = copy
    p1 = {}
    for h in range(chunks):
        for k in range(1, ndp):
            p2[h, k].wait_recv()
        p2[h, 0].wait()
        for k in range(1, nshard):
            target = (me_s + k) % nshard
            r = target // nx
            x = target % nx
            for j in range(CAP):
                send1[h, k, j] = recv2[h][tab[o_row + r * CAP + j], x]
            copy = pltpu.make_async_remote_copy(
                send1.at[h, k], recv1[h].at[pl.ds(me_s * CAP, CAP)], p1_s.at[h, k], p1_r.at[h, k],
                device_id=(me_d, target), device_id_type=MESH)
            copy.start()
            p1[h, k] = copy
        for j in range(CAP):
            recv1[h][me_s * CAP + j] = recv2[h][tab[o_row + (me_s // nx) * CAP + j], me_s % nx]
    a_in.wait()
    outs = []
    for h in range(chunks):
        for k in range(1, nshard):
            p1[h, k].wait_recv()
        rows = pl.ds(h * SUB, SUB)
        for c in range(nbc):
            scale = jnp.concatenate([ad[pl.ds(c, 1), :]] * (block // 128), axis=1)
            out[rows, pl.ds(c * block, block)] = recv1[h][tab[o_final + c]] * scale
        copy = pltpu.make_async_copy(out.at[rows, :], update.at[rows, :], io_sem.at[1 + h])
        copy.start()
        outs.append(copy)
    for h in range(chunks):
        for k in range(1, ndp):
            p2[h, k].wait_send()
        for k in range(1, nshard):
            p1[h, k].wait_send()
        outs[h].wait()


def back(tab, way, adam, dims, block, rows_dev, columns):
    ndp, nshard, nx, nbr, nbc = dims
    chunks = rows_dev // SUB
    f32 = jnp.float32
    anywhere = pl.BlockSpec(memory_space=pl.ANY)
    dma = pltpu.SemaphoreType.DMA
    return pl.pallas_call(
        functools.partial(back_kernel, dims, block, chunks),
        out_shape=jax.ShapeDtypeStruct((rows_dev, columns), f32),
        in_specs=[pl.BlockSpec(memory_space=pltpu.SMEM), anywhere, anywhere],
        out_specs=anywhere,
        scratch_shapes=[
            [pltpu.VMEM((ndp, nx, SUB, block), f32) for _ in range(chunks)],
            pltpu.VMEM((chunks, nshard, CAP, SUB, block), f32),
            [pltpu.VMEM((nshard * CAP, SUB, block), f32) for _ in range(chunks)],
            pltpu.VMEM((rows_dev, columns), f32),
            pltpu.VMEM((nbc, 128), f32),
            dma((chunks, ndp)),
            dma((chunks, ndp)),
            dma((chunks, nshard)),
            dma((chunks, nshard)),
            dma((1 + chunks,)),
        ],
        compiler_params=pltpu.CompilerParams(
            collective_id=1, has_side_effects=True, vmem_limit_bytes=40 * MIB),
    )(tab, way, adam)


def local(grad_parts, moment, second, left_prev, right_prev, owners, newton_steps):
    ndp = lax.axis_size("dp")
    nshard = lax.axis_size("shard")
    my_dp = lax.axis_index("dp")
    my_shard = lax.axis_index("shard")
    _, rows_dev, columns = moment.shape
    block = left_prev.shape[-1]
    nx = block // (rows_dev * ndp)
    dims = (ndp, nshard, nx, nshard // nx, columns // block)
    tab = routes(owners, newton_steps, my_dp, my_shard, dims)
    gblk, mom, sec, adam = forward(tab, grad_parts[0], moment[0], second[0], dims, block)
    place = offsets(dims)[4]
    left, right, lroot, rroot, way, mom, sec = owner_step(
        tab, gblk.reshape(block, block), left_prev[0, 0, 0], right_prev[0, 0, 0], mom, sec, place)
    chunks = rows_dev // SUB
    update = back(tab, way.reshape(nx, ndp, chunks, SUB, block), adam, dims, block, rows_dev, columns)
    slots = (1, 1, 1, block, block)
    return (
        update[None],
        mom[None],
        sec[None],
        left.reshape(slots),
        right.reshape(slots),
        lroot.reshape(slots),
        rroot.reshape(slots),
    )


def solution(mesh):
    rows = P("shard", "dp", None)
    slots = P("dp", "shard", None, None, None)
    return jax.shard_map(
        local,
        mesh=mesh,
        in_specs=(P("dp", "shard", None), rows, rows, slots, slots, P(), P()),
        out_specs=(rows, rows, rows, slots, slots, slots, slots),
        check_vma=False,
    )
```

```python
import functools

import jax
import jax.numpy as jnp
from jax import lax
from jax.experimental import pallas as pl
from jax.experimental.pallas import tpu as pltpu
from jax.sharding import PartitionSpec as P

MESH = pl.DeviceIdType.MESH
CORES = 2
SUB = 8
CAP = 2
MIB = 1 << 20


def route_table(own, steps, my_dp, my_shard, dims):
    ndp, nshard, nx, nbr, nbc = dims
    count = nbr * nbc
    o_sends, o_rank, o_row, o_final, o_steps = offsets(dims)
    down = lax.broadcasted_iota(jnp.int32, (count, count), 0)
    across = lax.broadcasted_iota(jnp.int32, (count, count), 1)
    wide = jnp.broadcast_to(own, (count, count))

    def turned(row):
        return jnp.sum(jnp.where(down == across, jnp.broadcast_to(row, (count, count)), 0), axis=1, keepdims=True)

    owner = turned(own)
    earlier = jnp.where((owner == wide) & (across < down), 1, 0)
    rank = jnp.sum(earlier, axis=1, keepdims=True)
    sub = jnp.sum(jnp.where(across // nbc == down // nbc, earlier, 0), axis=1, keepdims=True)
    count_of = turned(steps)
    lane = lax.broadcasted_iota(jnp.int32, (count, 128), 1)
    block = lax.broadcasted_iota(jnp.int32, (count, 128), 0)

    def spread(column):
        return jnp.broadcast_to(column, (count, 128))

    owner, rank, sub, count_of = (spread(column) for column in (owner, rank, sub, count_of))
    row, column = block // nbc, block % nbc
    mine = jnp.where(owner == my_shard, 1, 0)
    here = jnp.where(row == my_shard // nx, 1, 0)
    slot = owner * CAP + sub
    place = row * CAP + sub
    key = jnp.where(lane < o_rank, slot, jnp.where(lane < o_row, rank + o_rank, jnp.where(
        lane < o_final, place + o_row, jnp.where(lane < o_steps, column + o_final, -1))))
    value = jnp.where(lane < o_rank, column, jnp.where(lane < o_row, place, jnp.where(
        lane < o_final, rank, slot)))
    chosen = jnp.where((lane < o_rank) | (lane >= o_final), here, mine)
    table = jnp.where(key == lane, value * chosen, 0)
    held = jnp.where(rank == my_dp, mine, 0)
    table = table + jnp.where(lane == o_steps, held * count_of, jnp.where(lane == o_steps + 1, held, 0))
    return jnp.sum(table, axis=0, keepdims=True)


def offsets(dims):
    ndp, nshard, nx, nbr, nbc = dims
    sends = 0
    by_rank = sends + nshard * CAP
    by_row = by_rank + ndp
    finals = by_row + nbr * CAP
    steps = finals + nbc
    return sends, by_rank, by_row, finals, steps


def greet(peers):
    barrier = pltpu.get_barrier_semaphore()
    for peer in peers:
        pl.semaphore_signal(barrier, inc=1, device_id=peer, device_id_type=MESH)
    pl.semaphore_wait(barrier, len(peers))


def forward_kernel(dims, block, chunks, own, steps, grad, mom, sec,
                   gblk, mom_out, sec_out, adam_out, tab_out,
                   ibuf, tvec, tab, loc, pair, first_up, first_down, from_below, from_above,
                   gsel, mbuf, vbuf, send1, recv1, send2, asend, arecv, xsend, xrecv,
                   loc_sem, pair_s, pair_r, ring_s, ring_r, p1_s, p1_r, p2_s, p2_r,
                   a_s, a_r, x_s, x_r, io_sem, t_sem):
    ndp, nshard, nx, nbr, nbc = dims
    o_sends, o_rank, _, _, _ = offsets(dims)
    nz = ndp // CORES
    columns = nbc * block
    half = columns // 2
    rows_dev = SUB * chunks
    me_d = lax.axis_index("dp")
    me_s = lax.axis_index("shard")
    z = me_d // CORES
    core = me_d % CORES
    my_x = me_s % nx
    my_row = me_s // nx

    def zed(step):
        return (z + step) % nz

    def rows_of(zz, cc, h):
        return pl.ds(pl.multiple_of((zz * CORES + cc) * rows_dev + h * SUB, SUB), SUB)

    order = (2, 1, nz - 1, 0)
    loads = {}
    lists = [pltpu.make_async_copy(src, ibuf.at[i], t_sem.at[i]) for i, src in enumerate((own, steps))]
    for copy in lists:
        copy.start()
    for h in range(chunks):
        for q, step in enumerate(order):
            loads[h, q] = pltpu.make_async_copy(
                grad.at[rows_of(zed(step), core, h), :], loc.at[h, q], loc_sem.at[h, q])
            loads[h, q].start()
    m_in = pltpu.make_async_copy(mom, mbuf, io_sem.at[0])
    v_in = pltpu.make_async_copy(sec, vbuf, io_sem.at[1])
    m_in.start()
    v_in.start()

    dps = [((me_d + k) % ndp, me_s) for k in range(1, ndp)]
    shards = [(me_d, (me_s + k) % nshard) for k in range(1, nshard)]
    greet(dps + shards)

    sibling = (z * CORES + (1 - core), me_s)
    above = (zed(1) * CORES + core, me_s)
    below = (zed(nz - 1) * CORES + core, me_s)
    pairs = {}
    for h in range(chunks):
        for q, step in enumerate(order):
            pairs[h, q] = pltpu.make_async_remote_copy(
                grad.at[rows_of(zed(step), 1 - core, h), :], pair.at[h, q],
                pair_s.at[h, q], pair_r.at[h, q], device_id=sibling, device_id_type=MESH)
            pairs[h, q].start()

    for copy in lists:
        copy.wait()
    tvec[...] = route_table(ibuf[0], ibuf[1], me_d, me_s, dims)
    table_in = pltpu.make_async_copy(tvec, tab, t_sem.at[0])
    table_in.start()
    table_out = pltpu.make_async_copy(tvec, tab_out, t_sem.at[1])
    table_out.start()

    lo = pl.ds(0, half)
    hi = pl.ds(half, half)
    ring = {}

    def ring_send(h, index, src, dst, target):
        copy = pltpu.make_async_remote_copy(
            src, dst, ring_s.at[h, index], ring_r.at[h, index], device_id=target, device_id_type=MESH)
        copy.start()
        ring[h, index] = copy

    def merge(h, q):
        loads[h, q].wait()
        pairs[h, q].wait_recv()
        loc[h, q] = loc[h, q] + pair[h, q]

    def ring_one(h):
        merge(h, 0)
        ring_send(h, 0, loc.at[h, 0, :, lo], first_up.at[h], above)
        ring_send(h, 1, loc.at[h, 0, :, hi], first_down.at[h], below)
        merge(h, 1)
        ring_send(h, 2, loc.at[h, 1, :, hi], from_below.at[h, :, hi], above)
        merge(h, 2)
        ring_send(h, 3, loc.at[h, 2, :, lo], from_above.at[h, :, lo], below)
        merge(h, 3)

    def ring_two(h):
        ring[h, 0].wait_recv()
        loc[h, 1, :, lo] = loc[h, 1, :, lo] + first_up[h]
        ring_send(h, 4, loc.at[h, 1, :, lo], from_below.at[h, :, lo], above)
        ring[h, 1].wait_recv()
        loc[h, 2, :, hi] = loc[h, 2, :, hi] + first_down[h]
        ring_send(h, 5, loc.at[h, 2, :, hi], from_above.at[h, :, hi], below)

    def ring_end(h):
        for index in range(2, 6):
            ring[h, index].wait_recv()
        for c in range(nbc):
            cols = pl.ds(c * block, block)
            gsel[h, c] = (loc[h, 3, :, cols] + from_below[h, :, cols]) + from_above[h, :, cols]

    p1 = {}

    def exchange_shards(h):
        for k in range(1, nshard):
            target = (me_s + k) % nshard
            for j in range(CAP):
                send1[h, k, j] = gsel[h, tab[0, o_sends + target * CAP + j]]
            copy = pltpu.make_async_remote_copy(
                send1.at[h, k], recv1[h].at[me_s], p1_s.at[h, k], p1_r.at[h, k],
                device_id=(me_d, target), device_id_type=MESH)
            copy.start()
            p1[h, k] = copy
        for j in range(CAP):
            recv1[h][me_s, j] = gsel[h, tab[0, o_sends + me_s * CAP + j]]

    p2 = {}

    def exchange_dp(h):
        for k in range(1, nshard):
            p1[h, k].wait_recv()
        for k in list(range(1, ndp)) + [0]:
            target = (me_d + k) % ndp
            place = tab[0, o_rank + target]
            r = place // CAP
            j = place % CAP
            for x in range(nx):
                send2[h, k, x] = recv1[h][r * nx + x, j]
            if k:
                copy = pltpu.make_async_remote_copy(
                    send2.at[h, k], gblk.at[:, me_d, h], p2_s.at[h, k], p2_r.at[h, k],
                    device_id=(target, me_s), device_id_type=MESH)
            else:
                copy = pltpu.make_async_copy(send2.at[h, 0], gblk.at[:, me_d, h], p2_s.at[h, 0])
            copy.start()
            p2[h, k] = copy

    def adam_rows(h):
        rows = pl.ds(h * SUB, SUB)
        for c in range(nbc):
            cols = pl.ds(c * block, block)
            g = gsel[h, c]
            m = 0.9 * mbuf[rows, cols] + 0.1 * g
            v = 0.99 * vbuf[rows, cols] + 0.01 * g * g
            mbuf[rows, cols] = m
            vbuf[rows, cols] = v
            a = m / (jnp.sqrt(v) + 1e-08)
            sq = jnp.sum(a * a, axis=0, keepdims=True)
            part = sq[:, 0:128]
            for t in range(1, block // 128):
                part = part + sq[:, t * 128:(t + 1) * 128]
            if h == 0:
                asend[pl.ds(c, 1), :] = part
            else:
                asend[pl.ds(c, 1), :] = asend[pl.ds(c, 1), :] + part

    ring_one(0)
    ring_two(0)
    for h in range(1, chunks):
        ring_one(h)
    m_in.wait()
    v_in.wait()
    table_in.wait()
    ring_end(0)
    exchange_shards(0)
    adam_rows(0)
    for h in range(1, chunks):
        ring_two(h)
        ring_end(h)
        exchange_shards(h)
        exchange_dp(h - 1)
        adam_rows(h)

    m_out = pltpu.make_async_copy(mbuf, mom_out, io_sem.at[0])
    v_out = pltpu.make_async_copy(vbuf, sec_out, io_sem.at[1])
    m_out.start()
    v_out.start()
    acopies = []
    for k in range(1, ndp):
        copy = pltpu.make_async_remote_copy(
            asend, arecv.at[k], a_s.at[k], a_r.at[k],
            device_id=((me_d + k) % ndp, me_s), device_id_type=MESH)
        copy.start()
        acopies.append(copy)
    exchange_dp(chunks - 1)
    total = asend[...]
    for k in range(1, ndp):
        acopies[k - 1].wait_recv()
        total = total + arecv[k]
    xsend[...] = total
    xcopies = []
    for k in range(1, nx):
        copy = pltpu.make_async_remote_copy(
            xsend, xrecv.at[k], x_s.at[k], x_r.at[k],
            device_id=(me_d, my_row * nx + (my_x + k) % nx), device_id_type=MESH)
        copy.start()
        xcopies.append(copy)
    for k in range(1, nx):
        xcopies[k - 1].wait_recv()
        total = total + xrecv[k]
    summed = jnp.sum(total, axis=1, keepdims=True)
    arecv[0] = jnp.broadcast_to(jnp.sqrt(summed), arecv.shape[1:])
    a_out = pltpu.make_async_copy(arecv.at[0], adam_out, io_sem.at[2])
    a_out.start()

    for h in range(chunks):
        for q in range(len(order)):
            pairs[h, q].wait_send()
        for index in range(6):
            ring[h, index].wait_send()
        for k in range(1, nshard):
            p1[h, k].wait_send()
        for k in range(1, ndp):
            p2[h, k].wait_send()
            p2[h, k].wait_recv()
        p2[h, 0].wait()
    for copy in acopies + xcopies:
        copy.wait_send()
    m_out.wait()
    v_out.wait()
    a_out.wait()
    table_out.wait()


def forward(own, steps, grad, mom, sec, dims, block):
    ndp, nshard, nx, nbr, nbc = dims
    rows_dev, columns = mom.shape
    chunks = rows_dev // SUB
    half = columns // 2
    f32 = jnp.float32
    anywhere = pl.BlockSpec(memory_space=pltpu.HBM)
    dma = pltpu.SemaphoreType.DMA
    body = functools.partial(forward_kernel, dims, block, chunks)
    return pl.pallas_call(
        body,
        out_shape=(
            jax.ShapeDtypeStruct((nx, ndp, chunks, SUB, block), f32),
            jax.ShapeDtypeStruct((rows_dev, columns), f32),
            jax.ShapeDtypeStruct((rows_dev, columns), f32),
            jax.ShapeDtypeStruct((nbc, 128), f32),
            jax.ShapeDtypeStruct((1, 128), jnp.int32),
        ),
        in_specs=[anywhere] * 5,
        out_specs=(anywhere,) * 5,
        scratch_shapes=[
            pltpu.VMEM((2, 1, nbr * nbc), jnp.int32),
            pltpu.VMEM((1, 128), jnp.int32),
            pltpu.SMEM((1, 128), jnp.int32),
            pltpu.VMEM((chunks, 4, SUB, columns), f32),
            pltpu.VMEM((chunks, 4, SUB, columns), f32),
            pltpu.VMEM((chunks, SUB, half), f32),
            pltpu.VMEM((chunks, SUB, half), f32),
            pltpu.VMEM((chunks, SUB, columns), f32),
            pltpu.VMEM((chunks, SUB, columns), f32),
            pltpu.VMEM((chunks, nbc, SUB, block), f32),
            pltpu.VMEM((rows_dev, columns), f32),
            pltpu.VMEM((rows_dev, columns), f32),
            pltpu.VMEM((chunks, nshard, CAP, SUB, block), f32),
            [pltpu.VMEM((nshard, CAP, SUB, block), f32) for _ in range(chunks)],
            pltpu.VMEM((chunks, ndp, nx, SUB, block), f32),
            pltpu.VMEM((nbc, 128), f32),
            pltpu.VMEM((ndp, nbc, 128), f32),
            pltpu.VMEM((nbc, 128), f32),
            pltpu.VMEM((nx, nbc, 128), f32),
            dma((chunks, 4)),
            dma((chunks, 4)),
            dma((chunks, 4)),
            dma((chunks, 6)),
            dma((chunks, 6)),
            dma((chunks, nshard)),
            dma((chunks, nshard)),
            dma((chunks, ndp)),
            dma((chunks, ndp)),
            dma((ndp,)),
            dma((ndp,)),
            dma((nx,)),
            dma((nx,)),
            dma((3,)),
            dma((2,)),
        ],
        compiler_params=pltpu.CompilerParams(
            collective_id=0, has_side_effects=True, vmem_limit_bytes=58 * MIB),
    )(own, steps, grad, mom, sec)


def split(value):
    high = value.astype(jnp.bfloat16)
    low = (value - high.astype(jnp.float32)).astype(jnp.bfloat16)
    return high, low


def dot(left, right, axes=((1,), (0,))):
    return lax.dot_general(left, right, (axes, ((), ())), preferred_element_type=jnp.float32)


def product(first, second_factor):
    return dot(first[0], second_factor[0]) + (
        dot(first[0], second_factor[1]) + dot(first[1], second_factor[0]))


def mirrored(top, corner):
    half = corner.shape[0]
    return jnp.concatenate([top, jnp.concatenate([top[:, half:].T, corner], axis=1)], axis=0)


def gram(value, axes):
    cross = dot(value[0], value[1], axes)
    return dot(value[0], value[0], axes) + (cross + cross.T)


def square_of(value):
    high, low = value
    half = high.shape[0] // 2
    cross = dot(high, low)
    top = dot(high[:half], high) + (
        cross[:half] + jnp.concatenate([cross[:half, :half].T, cross[half:, :half].T], axis=1))
    corner = dot(high[half:], high[:, half:]) + (cross[half:, half:] + cross[half:, half:].T)
    return mirrored(top, corner)


def even_product(first, second_factor):
    half = first[0].shape[0] // 2
    top = product((first[0][:half], first[1][:half]), second_factor)
    corner = product(
        (first[0][half:], first[1][half:]), (second_factor[0][:, half:], second_factor[1][:, half:]))
    return mirrored(top, corner)


def owner_kernel(step_place, tab, gblk, left_prev, right_prev, mom, sec,
                 left_out, right_out, lroot_out, rroot_out, mom_out, sec_out,
                 g_ref, stat, root, mbuf, vbuf, sem, io_sem):
    taken = tab[0, step_place + 1]
    size = g_ref.shape[0]
    g_in = pltpu.make_async_copy(gblk, g_ref, sem.at[0])
    ins = [pltpu.make_async_copy(prev, stat.at[i], sem.at[1 + i])
           for i, prev in enumerate((left_prev, right_prev))]
    g_in.start()
    for copy in ins:
        copy.start()
    moves = [pltpu.make_async_copy(src, dst, io_sem.at[i])
             for i, (src, dst) in enumerate(((mom, mbuf), (sec, vbuf)))]
    for copy in moves:
        copy.start()
    g_in.wait()
    for copy in ins:
        copy.wait()
    for copy in moves:
        copy.wait()
    moves = [pltpu.make_async_copy(src, dst, io_sem.at[i])
             for i, (src, dst) in enumerate(((mbuf, mom_out), (vbuf, sec_out)))]
    for copy in moves:
        copy.start()
    stat_outs = [pltpu.make_async_copy(stat.at[i], out, sem.at[1 + i])
                 for i, out in enumerate((left_out, right_out))]
    root_outs = [pltpu.make_async_copy(root.at[i], out, sem.at[3 + i])
                 for i, out in enumerate((lroot_out, rroot_out))]
    two = range(2)

    @pl.when(taken == 0)
    def _():
        for i in two:
            stat[i] = jnp.zeros((size, size), jnp.float32)
            root[i] = jnp.zeros((size, size), jnp.float32)
            stat_outs[i].start()
            root_outs[i].start()
        for i in two:
            stat_outs[i].wait()
            root_outs[i].wait()

    @pl.when(taken != 0)
    def _():
        diagonal = lax.broadcasted_iota(jnp.int32, (size, size), 0) == lax.broadcasted_iota(
            jnp.int32, (size, size), 1)

        def complement(matrix):
            return split(jnp.where(diagonal, 1.25, 0.0) - 0.25 * matrix)

        g = split(g_ref[...])
        grams = [gram(g, axes) for axes in (((1,), (1,)), ((0,), (0,)))]
        for i in two:
            stat[i] = 0.95 * stat[i] + grams[i]
            stat_outs[i].start()
        scales, matrix = [], []
        for i in two:
            shifted = stat[i] + jnp.where(diagonal, 0.0001, 0.0)
            scale = 2.5 / jnp.sqrt(jnp.full((1, 1), jnp.sum(shifted * shifted)))
            scales.append(jnp.sqrt(jnp.sqrt(scale)))
            matrix.append(scale * shifted)
        factor = [complement(matrix[i]) for i in two]
        square = [split(square_of(factor[i])) for i in two]
        fourth = [split(square_of(square[i])) for i in two]
        matrix = [even_product(fourth[i], split(matrix[i])) for i in two]
        after = [complement(matrix[i]) for i in two]
        square = [split(square_of(after[i])) for i in two]
        current = [even_product(factor[i], after[i]) for i in two]
        fourth = [split(square_of(square[i])) for i in two]
        matrix = [even_product(fourth[i], split(matrix[i])) for i in two]
        more = tab[0, step_place] > 2
        for i in two:
            third = even_product(split(current[i]), complement(matrix[i]))
            root[i] = scales[i] * jnp.where(more, third, current[i])
            root_outs[i].start()
        for i in two:
            stat_outs[i].wait()
            root_outs[i].wait()

    for copy in moves:
        copy.wait()


def owner_step(tab, gblk, left_prev, right_prev, mom, sec, step_place):
    size = gblk.shape[0]
    f32 = jnp.float32
    square = jax.ShapeDtypeStruct((size, size), f32)
    rows = jax.ShapeDtypeStruct(mom.shape, f32)
    hbm = pl.BlockSpec(memory_space=pltpu.HBM)
    return pl.pallas_call(
        functools.partial(owner_kernel, step_place),
        out_shape=(square,) * 4 + (rows,) * 2,
        in_specs=[pl.BlockSpec(memory_space=pltpu.SMEM)] + [hbm] * 5,
        out_specs=(hbm,) * 6,
        scratch_shapes=[
            pltpu.VMEM((size, size), f32),
            pltpu.VMEM((2, size, size), f32),
            pltpu.VMEM((2, size, size), f32),
            pltpu.VMEM(mom.shape, f32),
            pltpu.VMEM(mom.shape, f32),
            pltpu.SemaphoreType.DMA((5,)),
            pltpu.SemaphoreType.DMA((2,)),
        ],
        compiler_params=pltpu.CompilerParams(vmem_limit_bytes=58 * MIB),
        cost_estimate=pl.CostEstimate(
            flops=100 * size ** 3, bytes_accessed=36 * size * size, transcendentals=0),
    )(tab, gblk, left_prev, right_prev, mom, sec)


def back_kernel(dims, block, rows_dev, tab, gblk, lroot, rroot, adam, update,
                gbuf, lbuf, rbuf, pbuf, recv2, send1, recv1, out, ad, fac, facs,
                p2_s, p2_r, f_s, f_r, p1_s, p1_r, io_sem):
    ndp, nshard, nx, nbr, nbc = dims
    _, _, o_row, o_final, _ = offsets(dims)
    me_d = lax.axis_index("dp")
    me_s = lax.axis_index("shard")
    my_x = me_s % nx
    my_row = me_s // nx
    ins = [pltpu.make_async_copy(src, dst, io_sem.at[i])
           for i, (src, dst) in enumerate(((gblk, gbuf), (rroot, rbuf), (lroot, lbuf), (adam, ad)))]
    for copy in ins:
        copy.start()
    dps = [((me_d + k) % ndp, me_s) for k in range(1, ndp)]
    shards = [(me_d, (me_s + k) % nshard) for k in range(1, nshard)]
    greet(dps + shards)
    for copy in ins:
        copy.wait()
    order = [q for q in range(nx // 2, 0, -1)] + [q for q in range(nx // 2 + 1, nx)] + [0]

    g = split(gbuf[...])
    right = split(rbuf[...])
    power = jnp.zeros((1, 1), jnp.float32)
    p2 = {}
    for q in order:
        x = (my_x + q) % nx
        span = ndp * rows_dev
        left = split(lbuf[pl.ds(pl.multiple_of(x * span, span), span), :])
        way = product(split(product(left, g)), right)
        pbuf[q] = way.reshape(ndp, rows_dev, block)
        power = power + jnp.sum(jnp.sum(way * way, axis=0, keepdims=True), axis=1, keepdims=True)
        for k in range(1, ndp):
            target = (me_d + k) % ndp
            copy = pltpu.make_async_remote_copy(
                pbuf.at[q, target], recv2[q].at[me_d], p2_s.at[q, k], p2_r.at[q, k],
                device_id=(target, me_s), device_id_type=MESH)
            copy.start()
            p2[q, k] = copy
        recv2[q][me_d] = pbuf[q, me_d]
    fac[...] = jnp.broadcast_to(1.0 / jnp.sqrt(power + 1e-12), fac.shape)
    facs[me_d] = fac[...]
    factors = []
    for k in range(1, ndp):
        copy = pltpu.make_async_remote_copy(
            fac, facs.at[me_d], f_s.at[k], f_r.at[k],
            device_id=((me_d + k) % ndp, me_s), device_id_type=MESH)
        copy.start()
        factors.append(copy)

    def scaled(q, row, j):
        rank = tab[0, o_row + row * CAP + j]
        by = jnp.concatenate([facs[rank]] * (block // 128), axis=1)
        return recv2[q][rank] * by

    p1 = {}
    for q in order:
        for k in range(1, ndp):
            p2[q, k].wait_recv()
        if q == order[0]:
            for copy in factors:
                copy.wait_recv()
        x = (my_x + q) % nx
        for w in range(nbr):
            row = (my_row + w) % nbr
            if q == 0 and w == 0:
                for j in range(CAP):
                    recv1[me_s * CAP + j] = scaled(q, row, j)
                continue
            for j in range(CAP):
                send1[q, w, j] = scaled(q, row, j)
            copy = pltpu.make_async_remote_copy(
                send1.at[q, w], recv1.at[pl.ds(me_s * CAP, CAP)], p1_s.at[q, w], p1_r.at[q, w],
                device_id=(me_d, row * nx + x), device_id_type=MESH)
            copy.start()
            p1[q, w] = copy
    for copy in p1.values():
        copy.wait_recv()
    for c in range(nbc):
        scale = jnp.concatenate([ad[pl.ds(c, 1), :]] * (block // 128), axis=1)
        out[:, pl.ds(c * block, block)] = recv1[tab[0, o_final + c]] * scale
    done = pltpu.make_async_copy(out, update, io_sem.at[0])
    done.start()
    for copy in list(p2.values()) + factors + list(p1.values()):
        copy.wait_send()
    done.wait()


def back(tab, gblk, lroot, rroot, adam, dims, block, rows_dev, columns):
    ndp, nshard, nx, nbr, nbc = dims
    f32 = jnp.float32
    hbm = pl.BlockSpec(memory_space=pltpu.HBM)
    dma = pltpu.SemaphoreType.DMA
    return pl.pallas_call(
        functools.partial(back_kernel, dims, block, rows_dev),
        out_shape=jax.ShapeDtypeStruct((rows_dev, columns), f32),
        in_specs=[pl.BlockSpec(memory_space=pltpu.SMEM)] + [hbm] * 4,
        out_specs=hbm,
        scratch_shapes=[
            pltpu.VMEM((block, block), f32),
            pltpu.VMEM((block, block), f32),
            pltpu.VMEM((block, block), f32),
            pltpu.VMEM((nx, ndp, rows_dev, block), f32),
            [pltpu.VMEM((ndp, rows_dev, block), f32) for _ in range(nx)],
            pltpu.VMEM((nx, nbr, CAP, rows_dev, block), f32),
            pltpu.VMEM((nshard * CAP, rows_dev, block), f32),
            pltpu.VMEM((rows_dev, columns), f32),
            pltpu.VMEM((nbc, 128), f32),
            pltpu.VMEM((rows_dev, 128), f32),
            pltpu.VMEM((ndp, rows_dev, 128), f32),
            dma((nx, ndp)),
            dma((nx, ndp)),
            dma((ndp,)),
            dma((ndp,)),
            dma((nx, nbr)),
            dma((nx, nbr)),
            dma((4,)),
        ],
        compiler_params=pltpu.CompilerParams(
            collective_id=1, has_side_effects=True, vmem_limit_bytes=58 * MIB),
    )(tab, gblk, lroot, rroot, adam)


def local(grad_parts, moment, second, left_prev, right_prev, owners, newton_steps):
    ndp = lax.axis_size("dp")
    nshard = lax.axis_size("shard")
    _, rows_dev, columns = moment.shape
    block = left_prev.shape[-1]
    nx = block // (rows_dev * ndp)
    dims = (ndp, nshard, nx, nshard // nx, columns // block)
    gblk, mom, sec, adam, tab = forward(
        owners[None], newton_steps[None], grad_parts[0], moment[0], second[0], dims, block)
    gblk = gblk.reshape(block, block)
    left, right, lroot, rroot, mom, sec = owner_step(
        tab, gblk, left_prev[0, 0, 0], right_prev[0, 0, 0], mom, sec, offsets(dims)[4])
    update = back(tab, gblk, lroot, rroot, adam, dims, block, rows_dev, columns)
    slots = (1, 1, 1, block, block)
    return (
        update[None],
        mom[None],
        sec[None],
        left.reshape(slots),
        right.reshape(slots),
        lroot.reshape(slots),
        rroot.reshape(slots),
    )


def solution(mesh):
    rows = P("shard", "dp", None)
    slots = P("dp", "shard", None, None, None)
    return jax.shard_map(
        local,
        mesh=mesh,
        in_specs=(P("dp", "shard", None), rows, rows, slots, slots, P(), P()),
        out_specs=(rows, rows, rows, slots, slots, slots, slots),
        check_vma=False,
    )
```

```python
import functools

import jax
import jax.numpy as jnp
from jax import lax
from jax.experimental import pallas as pl
from jax.experimental.pallas import tpu as pltpu
from jax.sharding import PartitionSpec as P

MESH = pl.DeviceIdType.MESH
CORES = 2
LANES = 128
CAP = 2
MIB = 1 << 20


def route_table(own, steps, my_dp, my_shard, dims):
    ndp, nshard, nx, nbr, nbc = dims
    count = nbr * nbc
    o_sends, o_rank, o_row, o_final, o_steps = offsets(dims)
    down = lax.broadcasted_iota(jnp.int32, (count, count), 0)
    across = lax.broadcasted_iota(jnp.int32, (count, count), 1)
    wide = jnp.broadcast_to(own, (count, count))

    def turned(row):
        return jnp.sum(jnp.where(down == across, jnp.broadcast_to(row, (count, count)), 0), axis=1, keepdims=True)

    owner = turned(own)
    earlier = jnp.where((owner == wide) & (across < down), 1, 0)
    rank = jnp.sum(earlier, axis=1, keepdims=True)
    sub = jnp.sum(jnp.where(across // nbc == down // nbc, earlier, 0), axis=1, keepdims=True)
    count_of = turned(steps)
    lane = lax.broadcasted_iota(jnp.int32, (count, 128), 1)
    block = lax.broadcasted_iota(jnp.int32, (count, 128), 0)

    def spread(column):
        return jnp.broadcast_to(column, (count, 128))

    owner, rank, sub, count_of = (spread(column) for column in (owner, rank, sub, count_of))
    row, column = block // nbc, block % nbc
    mine = jnp.where(owner == my_shard, 1, 0)
    here = jnp.where(row == my_shard // nx, 1, 0)
    slot = owner * CAP + sub
    place = row * CAP + sub
    key = jnp.where(lane < o_rank, slot, jnp.where(lane < o_row, rank + o_rank, jnp.where(
        lane < o_final, place + o_row, jnp.where(lane < o_steps, column + o_final, -1))))
    value = jnp.where(lane < o_rank, column, jnp.where(lane < o_row, place, jnp.where(
        lane < o_final, rank, slot)))
    chosen = jnp.where((lane < o_rank) | (lane >= o_final), here, mine)
    table = jnp.where(key == lane, value * chosen, 0)
    held = jnp.where(rank == my_dp, mine, 0)
    table = table + jnp.where(lane == o_steps, held * count_of, jnp.where(lane == o_steps + 1, held, 0))
    return jnp.sum(table, axis=0, keepdims=True)


def offsets(dims):
    ndp, nshard, nx, nbr, nbc = dims
    sends = 0
    by_rank = sends + nshard * CAP
    by_row = by_rank + ndp
    finals = by_row + nbr * CAP
    steps = finals + nbc
    return sends, by_rank, by_row, finals, steps


def signal(peers):
    barrier = pltpu.get_barrier_semaphore()
    for peer in peers:
        pl.semaphore_signal(barrier, inc=1, device_id=peer, device_id_type=MESH)


def await_peers(peers):
    pl.semaphore_wait(pltpu.get_barrier_semaphore(), len(peers))


def greet(peers):
    signal(peers)
    await_peers(peers)


def joined(chunked):
    return jnp.concatenate([chunked[t] for t in range(chunked.shape[0])], axis=1)


def far_first(count, width):
    def length(k):
        across, down = k % width, k // width
        high = count // width
        return min(across, width - across) + min(down, high - down)

    return sorted(range(1, count), key=lambda k: -length(k))


def dp_steps(ndp):
    nz = ndp // CORES
    steps = [(a, c) for a in range(nz) for c in range(CORES) if a or c]
    return sorted(steps, key=lambda k: -min(k[0], nz - k[0]))


def dp_peer(me_d, step, ndp):
    nz = ndp // CORES
    return (me_d // CORES + step[0]) % nz * CORES + (me_d % CORES + step[1]) % CORES


def forward_kernel(dims, block, own, steps, grad, mom, sec,
                   gblk, mom_out, sec_out, adam_out, tab_out,
                   ibuf, tvec, tab, loc, pair, acc, first_up, first_down, from_below, from_above,
                   gsel, mbuf, vbuf, send1, recv1, send2, asend,
                   loc_sem, pair_s, pair_r, ring_s, ring_r, p1_s, p1_r, p2_s, p2_r,
                   io_sem, t_sem):
    ndp, nshard, nx, nbr, nbc = dims
    o_sends, o_rank, _, _, _ = offsets(dims)
    nz = ndp // CORES
    chunks = block // LANES
    half = nbc // 2
    rows_dev = mom.shape[0]
    me_d = lax.axis_index("dp")
    me_s = lax.axis_index("shard")
    z = me_d // CORES
    core = me_d % CORES

    def zed(step):
        return (z + step) % nz

    def rows_of(zz, cc):
        return pl.ds(pl.multiple_of((zz * CORES + cc) * rows_dev, rows_dev), rows_dev)

    order = (2, 1, nz - 1, 0)
    loads = []
    lists = [pltpu.make_async_copy(src, ibuf.at[i], t_sem.at[i]) for i, src in enumerate((own, steps))]
    for copy in lists:
        copy.start()
    for q, step in enumerate(order):
        loads.append(pltpu.make_async_copy(
            grad.at[rows_of(zed(step), core), :], loc.at[q], loc_sem.at[q]))
        loads[q].start()
    m_in = pltpu.make_async_copy(mom, mbuf, io_sem.at[0])
    v_in = pltpu.make_async_copy(sec, vbuf, io_sem.at[1])
    m_in.start()
    v_in.start()

    z_steps = dp_steps(ndp)
    s_steps = far_first(nshard, nx)
    greet([(dp_peer(me_d, step, ndp), me_s) for step in z_steps]
          + [(me_d, shard_peer(me_s, k, dims)) for k in s_steps])

    sibling = (z * CORES + (1 - core), me_s)
    above = (zed(1) * CORES + core, me_s)
    below = (zed(nz - 1) * CORES + core, me_s)
    pairs = []
    for q, step in enumerate(order):
        pairs.append(pltpu.make_async_remote_copy(
            grad.at[rows_of(zed(step), 1 - core), :], pair.at[q],
            pair_s.at[q], pair_r.at[q], device_id=sibling, device_id_type=MESH))
        pairs[q].start()

    for copy in lists:
        copy.wait()
    tvec[...] = route_table(ibuf[0], ibuf[1], me_d, me_s, dims)
    table_in = pltpu.make_async_copy(tvec, tab, t_sem.at[0])
    table_in.start()
    table_out = pltpu.make_async_copy(tvec, tab_out, t_sem.at[1])
    table_out.start()

    lo = pl.ds(0, half)
    hi = pl.ds(half, half)
    ring = {}

    def ring_send(t, index, src, dst, target):
        copy = pltpu.make_async_remote_copy(
            src, dst, ring_s.at[t, index], ring_r.at[t, index], device_id=target, device_id_type=MESH)
        copy.start()
        ring[t, index] = copy

    def merge(t, q):
        if t == 0:
            loads[q].wait()
            pairs[q].wait_recv()
        for c in range(nbc):
            cols = pl.ds(c * block + t * LANES, LANES)
            acc[t, q, c] = loc[q, :, cols] + pair[q, :, cols]

    def ring_one(t):
        merge(t, 0)
        ring_send(t, 0, acc.at[t, 0, lo], first_up.at[t], above)
        ring_send(t, 1, acc.at[t, 0, hi], first_down.at[t], below)
        merge(t, 1)
        ring_send(t, 2, acc.at[t, 1, hi], from_below.at[t, hi], above)
        merge(t, 2)
        ring_send(t, 3, acc.at[t, 2, lo], from_above.at[t, lo], below)
        merge(t, 3)

    def ring_two(t):
        ring[t, 0].wait_recv()
        acc[t, 1, lo] = acc[t, 1, lo] + first_up[t]
        ring_send(t, 4, acc.at[t, 1, lo], from_below.at[t, lo], above)
        ring[t, 1].wait_recv()
        acc[t, 2, hi] = acc[t, 2, hi] + first_down[t]
        ring_send(t, 5, acc.at[t, 2, hi], from_above.at[t, hi], below)

    def ring_end(t):
        for index in range(2, 6):
            ring[t, index].wait_recv()
        gsel[t] = (acc[t, 3] + from_below[t]) + from_above[t]

    p1 = {}

    def exchange_shards(t):
        for k in s_steps:
            target = shard_peer(me_s, k, dims)
            for j in range(CAP):
                send1[t, k, j] = gsel[t, tab[0, o_sends + target * CAP + j]]
            copy = pltpu.make_async_remote_copy(
                send1.at[t, k], recv1[t].at[me_s], p1_s.at[t, k], p1_r.at[t, k],
                device_id=(me_d, target), device_id_type=MESH)
            copy.start()
            p1[t, k] = copy
        for j in range(CAP):
            recv1[t][me_s, j] = gsel[t, tab[0, o_sends + me_s * CAP + j]]

    p2 = {}

    def exchange_dp(t):
        for k in s_steps:
            p1[t, k].wait_recv()
        for k, step in enumerate(z_steps + [(0, 0)]):
            target = dp_peer(me_d, step, ndp)
            place = tab[0, o_rank + target]
            r = place // CAP
            j = place % CAP
            for x in range(nx):
                send2[t, k, x] = recv1[t][r * nx + x, j]
            if k < len(z_steps):
                copy = pltpu.make_async_remote_copy(
                    send2.at[t, k], gblk.at[t, :, me_d], p2_s.at[t, k], p2_r.at[t, k],
                    device_id=(target, me_s), device_id_type=MESH)
            else:
                copy = pltpu.make_async_copy(send2.at[t, k], gblk.at[t, :, me_d], p2_s.at[t, k])
            copy.start()
            p2[t, k] = copy

    def adam_rows(t):
        for c in range(nbc):
            cols = pl.ds(c * block + t * LANES, LANES)
            g = gsel[t, c]
            m = 0.9 * mbuf[:, cols] + 0.1 * g
            v = 0.99 * vbuf[:, cols] + 0.01 * g * g
            mbuf[:, cols] = m
            vbuf[:, cols] = v
            a = m / (jnp.sqrt(v) + 1e-08)
            part = jnp.sum(a * a, axis=0, keepdims=True)
            if t == 0:
                asend[pl.ds(c, 1), :] = part
            else:
                asend[pl.ds(c, 1), :] = asend[pl.ds(c, 1), :] + part

    def shards_out(t):
        if t == 0:
            table_in.wait()
        ring_end(t)
        exchange_shards(t)

    ring_one(0)
    for t in range(1, chunks):
        ring_one(t)
        ring_two(t - 1)
        if t >= 2:
            shards_out(t - 2)
    ring_two(chunks - 1)
    for t in range(max(chunks - 2, 0), chunks):
        shards_out(t)
        if t > max(chunks - 2, 0):
            exchange_dp(t - (chunks - 1))
    m_in.wait()
    v_in.wait()
    for t in range(chunks):
        adam_rows(t)
        if t + 1 < chunks:
            exchange_dp(t + 1)

    m_out = pltpu.make_async_copy(mbuf, mom_out, io_sem.at[0])
    v_out = pltpu.make_async_copy(vbuf, sec_out, io_sem.at[1])
    a_out = pltpu.make_async_copy(asend, adam_out, io_sem.at[2])
    for copy in (m_out, v_out, a_out):
        copy.start()

    for copy in pairs + list(ring.values()) + list(p1.values()):
        copy.wait_send()
    for (t, k), copy in p2.items():
        if k < len(z_steps):
            copy.wait_send()
            copy.wait_recv()
        else:
            copy.wait()
    m_out.wait()
    v_out.wait()
    a_out.wait()
    table_out.wait()


def shard_peer(me_s, k, dims):
    _, _, nx, nbr, _ = dims
    return (me_s // nx + k // nx) % nbr * nx + (me_s % nx + k % nx) % nx


def forward(own, steps, grad, mom, sec, dims, block):
    ndp, nshard, nx, nbr, nbc = dims
    rows_dev, columns = mom.shape
    chunks = block // LANES
    f32 = jnp.float32
    hbm = pl.BlockSpec(memory_space=pltpu.HBM)
    dma = pltpu.SemaphoreType.DMA
    piece = (rows_dev, LANES)
    return pl.pallas_call(
        functools.partial(forward_kernel, dims, block),
        out_shape=(
            jax.ShapeDtypeStruct((chunks, nx, ndp) + piece, f32),
            jax.ShapeDtypeStruct((rows_dev, columns), f32),
            jax.ShapeDtypeStruct((rows_dev, columns), f32),
            jax.ShapeDtypeStruct((nbc, LANES), f32),
            jax.ShapeDtypeStruct((1, LANES), jnp.int32),
        ),
        in_specs=[hbm] * 5,
        out_specs=(hbm,) * 5,
        scratch_shapes=[
            pltpu.VMEM((2, 1, nbr * nbc), jnp.int32),
            pltpu.VMEM((1, LANES), jnp.int32),
            pltpu.SMEM((1, LANES), jnp.int32),
            pltpu.VMEM((4, rows_dev, columns), f32),
            pltpu.VMEM((4, rows_dev, columns), f32),
            pltpu.VMEM((chunks, 4, nbc) + piece, f32),
            pltpu.VMEM((chunks, nbc // 2) + piece, f32),
            pltpu.VMEM((chunks, nbc // 2) + piece, f32),
            pltpu.VMEM((chunks, nbc) + piece, f32),
            pltpu.VMEM((chunks, nbc) + piece, f32),
            pltpu.VMEM((chunks, nbc) + piece, f32),
            pltpu.VMEM((rows_dev, columns), f32),
            pltpu.VMEM((rows_dev, columns), f32),
            pltpu.VMEM((chunks, nshard, CAP) + piece, f32),
            [pltpu.VMEM((nshard, CAP) + piece, f32) for _ in range(chunks)],
            pltpu.VMEM((chunks, ndp, nx) + piece, f32),
            pltpu.VMEM((nbc, LANES), f32),
            dma((4,)),
            dma((4,)),
            dma((4,)),
            dma((chunks, 6)),
            dma((chunks, 6)),
            dma((chunks, nshard)),
            dma((chunks, nshard)),
            dma((chunks, ndp)),
            dma((chunks, ndp)),
            dma((3,)),
            dma((2,)),
        ],
        compiler_params=pltpu.CompilerParams(
            collective_id=0, has_side_effects=True, vmem_limit_bytes=58 * MIB),
    )(own, steps, grad, mom, sec)


def split(value):
    high = value.astype(jnp.bfloat16)
    low = (value - high.astype(jnp.float32)).astype(jnp.bfloat16)
    return high, low


def dot(left, right, axes=((1,), (0,))):
    return lax.dot_general(left, right, (axes, ((), ())), preferred_element_type=jnp.float32)


def product(first, second_factor):
    return dot(first[0], second_factor[0]) + (
        dot(first[0], second_factor[1]) + dot(first[1], second_factor[0]))


def mirrored(top, corner):
    half = corner.shape[0]
    return jnp.concatenate([top, jnp.concatenate([top[:, half:].T, corner], axis=1)], axis=0)


def gram(value, axes):
    cross = dot(value[0], value[1], axes)
    return dot(value[0], value[0], axes) + (cross + cross.T)


def square_of(value):
    high, low = value
    half = high.shape[0] // 2
    cross = dot(high, low)
    top = dot(high[:half], high) + (
        cross[:half] + jnp.concatenate([cross[:half, :half].T, cross[half:, :half].T], axis=1))
    corner = dot(high[half:], high[:, half:]) + (cross[half:, half:] + cross[half:, half:].T)
    return mirrored(top, corner)


def even_product(first, second_factor):
    half = first[0].shape[0] // 2
    top = product((first[0][:half], first[1][:half]), second_factor)
    corner = product(
        (first[0][half:], first[1][half:]), (second_factor[0][:, half:], second_factor[1][:, half:]))
    return mirrored(top, corner)


def owner_kernel(step_place, tab, gblk, left_prev, right_prev, mom, sec,
                 left_out, right_out, lroot_out, rroot_out, mom_out, sec_out,
                 g_ref, stat, root, mbuf, vbuf, sem, io_sem):
    taken = tab[0, step_place + 1]
    size = g_ref.shape[1]
    g_in = pltpu.make_async_copy(gblk, g_ref, sem.at[0])
    ins = [pltpu.make_async_copy(prev, stat.at[i], sem.at[1 + i])
           for i, prev in enumerate((left_prev, right_prev))]
    g_in.start()
    for copy in ins:
        copy.start()
    moves = [pltpu.make_async_copy(src, dst, io_sem.at[i])
             for i, (src, dst) in enumerate(((mom, mbuf), (sec, vbuf)))]
    for copy in moves:
        copy.start()
    g_in.wait()
    for copy in ins:
        copy.wait()
    for copy in moves:
        copy.wait()
    moves = [pltpu.make_async_copy(src, dst, io_sem.at[i])
             for i, (src, dst) in enumerate(((mbuf, mom_out), (vbuf, sec_out)))]
    for copy in moves:
        copy.start()
    stat_outs = [pltpu.make_async_copy(stat.at[i], out, sem.at[1 + i])
                 for i, out in enumerate((left_out, right_out))]
    root_outs = [pltpu.make_async_copy(root.at[i], out, sem.at[3 + i])
                 for i, out in enumerate((lroot_out, rroot_out))]
    two = range(2)

    @pl.when(taken == 0)
    def _():
        for i in two:
            stat[i] = jnp.zeros((size, size), jnp.float32)
            root[i] = jnp.zeros((size, size), jnp.float32)
            stat_outs[i].start()
            root_outs[i].start()
        for i in two:
            stat_outs[i].wait()
            root_outs[i].wait()

    @pl.when(taken != 0)
    def _():
        diagonal = lax.broadcasted_iota(jnp.int32, (size, size), 0) == lax.broadcasted_iota(
            jnp.int32, (size, size), 1)

        def complement(matrix):
            return split(jnp.where(diagonal, 1.25, 0.0) - 0.25 * matrix)

        g = split(joined(g_ref))
        grams = [gram(g, axes) for axes in (((1,), (1,)), ((0,), (0,)))]
        for i in two:
            stat[i] = 0.95 * stat[i] + grams[i]
            stat_outs[i].start()
        scales, matrix = [], []
        for i in two:
            shifted = stat[i] + jnp.where(diagonal, 0.0001, 0.0)
            scale = 2.5 / jnp.sqrt(jnp.full((1, 1), jnp.sum(shifted * shifted)))
            scales.append(jnp.sqrt(jnp.sqrt(scale)))
            matrix.append(scale * shifted)
        factor = [complement(matrix[i]) for i in two]
        square = [split(square_of(factor[i])) for i in two]
        fourth = [split(square_of(square[i])) for i in two]
        matrix = [even_product(fourth[i], split(matrix[i])) for i in two]
        after = [complement(matrix[i]) for i in two]
        square = [split(square_of(after[i])) for i in two]
        current = [even_product(factor[i], after[i]) for i in two]
        fourth = [split(square_of(square[i])) for i in two]
        matrix = [even_product(fourth[i], split(matrix[i])) for i in two]
        more = tab[0, step_place] > 2
        for i in two:
            third = even_product(split(current[i]), complement(matrix[i]))
            root[i] = scales[i] * jnp.where(more, third, current[i])
            root_outs[i].start()
        for i in two:
            stat_outs[i].wait()
            root_outs[i].wait()

    for copy in moves:
        copy.wait()


def owner_step(tab, gblk, left_prev, right_prev, mom, sec, step_place):
    size = gblk.shape[1]
    f32 = jnp.float32
    square = jax.ShapeDtypeStruct((size, size), f32)
    rows = jax.ShapeDtypeStruct(mom.shape, f32)
    hbm = pl.BlockSpec(memory_space=pltpu.HBM)
    return pl.pallas_call(
        functools.partial(owner_kernel, step_place),
        out_shape=(square,) * 4 + (rows,) * 2,
        in_specs=[pl.BlockSpec(memory_space=pltpu.SMEM)] + [hbm] * 5,
        out_specs=(hbm,) * 6,
        scratch_shapes=[
            pltpu.VMEM(gblk.shape, f32),
            pltpu.VMEM((2, size, size), f32),
            pltpu.VMEM((2, size, size), f32),
            pltpu.VMEM(mom.shape, f32),
            pltpu.VMEM(mom.shape, f32),
            pltpu.SemaphoreType.DMA((5,)),
            pltpu.SemaphoreType.DMA((2,)),
        ],
        compiler_params=pltpu.CompilerParams(vmem_limit_bytes=58 * MIB),
        cost_estimate=pl.CostEstimate(
            flops=100 * size ** 3, bytes_accessed=36 * size * size, transcendentals=0),
    )(tab, gblk, left_prev, right_prev, mom, sec)


def back_kernel(dims, block, rows_dev, tab, gblk, lroot, rroot, adam, update,
                gbuf, lbuf, rbuf, pbuf, recv2, send1, recv1, out, asend, arecv, xsend, xrecv,
                p2_s, p2_r, a_s, a_r, x_s, x_r, p1_s, p1_r, io_sem):
    ndp, nshard, nx, nbr, nbc = dims
    _, _, o_row, o_final, _ = offsets(dims)
    chunks = block // LANES
    me_d = lax.axis_index("dp")
    me_s = lax.axis_index("shard")
    ins = [pltpu.make_async_copy(src, dst, io_sem.at[i])
           for i, (src, dst) in enumerate(((lroot, lbuf), (gblk, gbuf), (rroot, rbuf), (adam, asend)))]
    for copy in ins:
        copy.start()
    z_steps = dp_steps(ndp)
    s_steps = far_first(nshard, nx)
    peers = [(dp_peer(me_d, step, ndp), me_s) for step in z_steps] + [
        (me_d, shard_peer(me_s, k, dims)) for k in s_steps]
    signal(peers)
    for copy in ins:
        copy.wait()
    turned = split(product(split(lbuf[...]), split(joined(gbuf))))
    way = product(turned, split(rbuf[...]))
    power = jnp.sum(jnp.sum(way * way, axis=0, keepdims=True), axis=1, keepdims=True)
    way = way * (1.0 / jnp.sqrt(power + 1e-12))
    for t in range(chunks):
        for x in range(nx):
            for d in range(ndp):
                top = (x * ndp + d) * rows_dev
                pbuf[t, d, x] = way[top:top + rows_dev, t * LANES:(t + 1) * LANES]
    await_peers(peers)

    acopies = []
    for k, step in enumerate(z_steps):
        copy = pltpu.make_async_remote_copy(
            asend, arecv.at[k], a_s.at[k], a_r.at[k],
            device_id=(dp_peer(me_d, step, ndp), me_s), device_id_type=MESH)
        copy.start()
        acopies.append(copy)
    p2 = {}
    for t in range(chunks):
        for k, step in enumerate(z_steps):
            target = dp_peer(me_d, step, ndp)
            copy = pltpu.make_async_remote_copy(
                pbuf.at[t, target], recv2[t].at[me_d], p2_s.at[t, k], p2_r.at[t, k],
                device_id=(target, me_s), device_id_type=MESH)
            copy.start()
            p2[t, k] = copy
        recv2[t][me_d] = pbuf[t, me_d]
    total = asend[...]
    for k, copy in enumerate(acopies):
        copy.wait_recv()
        total = total + arecv[k]
    xsend[...] = total
    xcopies = []
    for k in range(1, nx):
        copy = pltpu.make_async_remote_copy(
            xsend, xrecv.at[k], x_s.at[k], x_r.at[k],
            device_id=(me_d, me_s // nx * nx + (me_s % nx + k) % nx), device_id_type=MESH)
        copy.start()
        xcopies.append(copy)

    p1 = {}
    for t in range(chunks):
        for k in range(len(z_steps)):
            p2[t, k].wait_recv()

        def wanted(target, j):
            rank = tab[0, o_row + target // nx * CAP + j]
            return recv2[t][rank, target % nx]

        for k in s_steps:
            target = shard_peer(me_s, k, dims)
            for j in range(CAP):
                send1[t, k, j] = wanted(target, j)
            copy = pltpu.make_async_remote_copy(
                send1.at[t, k], recv1[t].at[pl.ds(me_s * CAP, CAP)], p1_s.at[t, k], p1_r.at[t, k],
                device_id=(me_d, target), device_id_type=MESH)
            copy.start()
            p1[t, k] = copy
        for j in range(CAP):
            recv1[t][me_s * CAP + j] = wanted(me_s, j)
    for k in range(1, nx):
        xcopies[k - 1].wait_recv()
        total = total + xrecv[k]
    ad = jnp.broadcast_to(jnp.sqrt(jnp.sum(total, axis=1, keepdims=True)), total.shape)
    for t in range(chunks):
        for k in s_steps:
            p1[t, k].wait_recv()
        for c in range(nbc):
            cols = pl.ds(c * block + t * LANES, LANES)
            out[:, cols] = recv1[t][tab[0, o_final + c]] * ad[c:c + 1, :]
    done = pltpu.make_async_copy(out, update, io_sem.at[0])
    done.start()
    for copy in list(p2.values()) + acopies + xcopies + list(p1.values()):
        copy.wait_send()
    done.wait()


def back(tab, gblk, lroot, rroot, adam, dims, block, rows_dev, columns):
    ndp, nshard, nx, nbr, nbc = dims
    chunks = block // LANES
    f32 = jnp.float32
    hbm = pl.BlockSpec(memory_space=pltpu.HBM)
    dma = pltpu.SemaphoreType.DMA
    piece = (rows_dev, LANES)
    return pl.pallas_call(
        functools.partial(back_kernel, dims, block, rows_dev),
        out_shape=jax.ShapeDtypeStruct((rows_dev, columns), f32),
        in_specs=[pl.BlockSpec(memory_space=pltpu.SMEM)] + [hbm] * 4,
        out_specs=pl.BlockSpec(memory_space=pl.ANY),
        scratch_shapes=[
            pltpu.VMEM(gblk.shape, f32),
            pltpu.VMEM((block, block), f32),
            pltpu.VMEM((block, block), f32),
            pltpu.VMEM((chunks, ndp, nx) + piece, f32),
            [pltpu.VMEM((ndp, nx) + piece, f32) for _ in range(chunks)],
            pltpu.VMEM((chunks, nshard, CAP) + piece, f32),
            [pltpu.VMEM((nshard * CAP,) + piece, f32) for _ in range(chunks)],
            pltpu.VMEM((rows_dev, columns), f32),
            pltpu.VMEM((nbc, LANES), f32),
            pltpu.VMEM((ndp, nbc, LANES), f32),
            pltpu.VMEM((nbc, LANES), f32),
            pltpu.VMEM((nx, nbc, LANES), f32),
            dma((chunks, ndp)),
            dma((chunks, ndp)),
            dma((ndp,)),
            dma((ndp,)),
            dma((nx,)),
            dma((nx,)),
            dma((chunks, nshard)),
            dma((chunks, nshard)),
            dma((4,)),
        ],
        compiler_params=pltpu.CompilerParams(
            collective_id=1, has_side_effects=True, vmem_limit_bytes=63 * MIB),
    )(tab, gblk, lroot, rroot, adam)


def local(grad_parts, moment, second, left_prev, right_prev, owners, newton_steps):
    ndp = lax.axis_size("dp")
    nshard = lax.axis_size("shard")
    _, rows_dev, columns = moment.shape
    block = left_prev.shape[-1]
    nx = block // (rows_dev * ndp)
    dims = (ndp, nshard, nx, nshard // nx, columns // block)
    gblk, mom, sec, adam, tab = forward(
        owners[None], newton_steps[None], grad_parts[0], moment[0], second[0], dims, block)
    gblk = gblk.reshape(block // LANES, block, LANES)
    left, right, lroot, rroot, mom, sec = owner_step(
        tab, gblk, left_prev[0, 0, 0], right_prev[0, 0, 0], mom, sec, offsets(dims)[4])
    update = back(tab, gblk, lroot, rroot, adam, dims, block, rows_dev, columns)
    slots = (1, 1, 1, block, block)
    return (
        update[None],
        mom[None],
        sec[None],
        left.reshape(slots),
        right.reshape(slots),
        lroot.reshape(slots),
        rroot.reshape(slots),
    )


def solution(mesh):
    rows = P("shard", "dp", None)
    slots = P("dp", "shard", None, None, None)
    return jax.shard_map(
        local,
        mesh=mesh,
        in_specs=(P("dp", "shard", None), rows, rows, slots, slots, P(), P()),
        out_specs=(rows, rows, rows, slots, slots, slots, slots),
        check_vma=False,
    )
```

```python
import functools

import jax
import jax.numpy as jnp
from jax import lax
from jax.experimental import pallas as pl
from jax.experimental.pallas import tpu as pltpu
from jax.sharding import PartitionSpec as P

MESH = pl.DeviceIdType.MESH
CORES = 2
LANES = 128
CAP = 2
MIB = 1 << 20


def route_table(own, steps, my_dp, my_shard, dims):
    ndp, nshard, nx, nbr, nbc = dims
    count = nbr * nbc
    o_sends, o_rank, o_row, o_final, o_steps = offsets(dims)
    down = lax.broadcasted_iota(jnp.int32, (count, count), 0)
    across = lax.broadcasted_iota(jnp.int32, (count, count), 1)
    wide = jnp.broadcast_to(own, (count, count))

    def turned(row):
        return jnp.sum(jnp.where(down == across, jnp.broadcast_to(row, (count, count)), 0), axis=1, keepdims=True)

    owner = turned(own)
    earlier = jnp.where((owner == wide) & (across < down), 1, 0)
    rank = jnp.sum(earlier, axis=1, keepdims=True)
    sub = jnp.sum(jnp.where(across // nbc == down // nbc, earlier, 0), axis=1, keepdims=True)
    count_of = turned(steps)
    lane = lax.broadcasted_iota(jnp.int32, (count, 128), 1)
    block = lax.broadcasted_iota(jnp.int32, (count, 128), 0)

    def spread(column):
        return jnp.broadcast_to(column, (count, 128))

    owner, rank, sub, count_of = (spread(column) for column in (owner, rank, sub, count_of))
    row, column = block // nbc, block % nbc
    mine = jnp.where(owner == my_shard, 1, 0)
    here = jnp.where(row == my_shard // nx, 1, 0)
    slot = owner * CAP + sub
    place = row * CAP + sub
    key = jnp.where(lane < o_rank, slot, jnp.where(lane < o_row, rank + o_rank, jnp.where(
        lane < o_final, place + o_row, jnp.where(lane < o_steps, column + o_final, -1))))
    value = jnp.where(lane < o_rank, column, jnp.where(lane < o_row, place, jnp.where(
        lane < o_final, rank, slot)))
    chosen = jnp.where((lane < o_rank) | (lane >= o_final), here, mine)
    table = jnp.where(key == lane, value * chosen, 0)
    held = jnp.where(rank == my_dp, mine, 0)
    table = table + jnp.where(lane == o_steps, held * count_of, jnp.where(lane == o_steps + 1, held, 0))
    return jnp.sum(table, axis=0, keepdims=True)


def offsets(dims):
    ndp, nshard, nx, nbr, nbc = dims
    sends = 0
    by_rank = sends + nshard * CAP
    by_row = by_rank + ndp
    finals = by_row + nbr * CAP
    steps = finals + nbc
    return sends, by_rank, by_row, finals, steps


def signal(peers):
    barrier = pltpu.get_barrier_semaphore()
    for peer in peers:
        pl.semaphore_signal(barrier, inc=1, device_id=peer, device_id_type=MESH)


def await_peers(peers):
    pl.semaphore_wait(pltpu.get_barrier_semaphore(), len(peers))


def greet(peers):
    signal(peers)
    await_peers(peers)


def joined(chunked):
    return jnp.concatenate([chunked[t] for t in range(chunked.shape[0])], axis=1)


def far_first(count, width):
    def length(k):
        across, down = k % width, k // width
        high = count // width
        return min(across, width - across) + min(down, high - down)

    return sorted(range(1, count), key=lambda k: -length(k))


def dp_steps(ndp):
    nz = ndp // CORES
    steps = [(a, c) for a in range(nz) for c in range(CORES) if a or c]
    return sorted(steps, key=lambda k: -min(k[0], nz - k[0]))


def dp_peer(me_d, step, ndp):
    nz = ndp // CORES
    return (me_d // CORES + step[0]) % nz * CORES + (me_d % CORES + step[1]) % CORES


def forward_kernel(dims, block, own, steps, grad, mom, sec,
                   gblk, mom_out, sec_out, adam_out, tab_out,
                   ibuf, tvec, tab, loc, pair, acc, first_up, first_down, from_below, from_above,
                   gsel, mbuf, vbuf, send1, recv1, send2, asend,
                   loc_sem, pair_s, pair_r, ring_s, ring_r, p1_s, p1_r, p2_s, p2_r,
                   io_sem, t_sem):
    ndp, nshard, nx, nbr, nbc = dims
    o_sends, o_rank, _, _, _ = offsets(dims)
    nz = ndp // CORES
    chunks = block // LANES
    half = nbc // 2
    rows_dev = mom.shape[0]
    me_d = lax.axis_index("dp")
    me_s = lax.axis_index("shard")
    z = me_d // CORES
    core = me_d % CORES

    def zed(step):
        return (z + step) % nz

    def rows_of(zz, cc):
        return pl.ds(pl.multiple_of((zz * CORES + cc) * rows_dev, rows_dev), rows_dev)

    order = (2, 1, nz - 1, 0)
    loads = []
    lists = [pltpu.make_async_copy(src, ibuf.at[i], t_sem.at[i]) for i, src in enumerate((own, steps))]
    for copy in lists:
        copy.start()
    for q, step in enumerate(order):
        loads.append(pltpu.make_async_copy(
            grad.at[rows_of(zed(step), core), :], loc.at[q], loc_sem.at[q]))
        loads[q].start()
    m_in = pltpu.make_async_copy(mom, mbuf, io_sem.at[0])
    v_in = pltpu.make_async_copy(sec, vbuf, io_sem.at[1])
    m_in.start()
    v_in.start()

    z_steps = dp_steps(ndp)
    s_steps = far_first(nshard, nx)
    greet([(dp_peer(me_d, step, ndp), me_s) for step in reversed(z_steps)]
          + [(me_d, shard_peer(me_s, k, dims)) for k in s_steps])

    sibling = (z * CORES + (1 - core), me_s)
    above = (zed(1) * CORES + core, me_s)
    below = (zed(nz - 1) * CORES + core, me_s)
    pairs = []
    for q, step in enumerate(order):
        pairs.append(pltpu.make_async_remote_copy(
            grad.at[rows_of(zed(step), 1 - core), :], pair.at[q],
            pair_s.at[q], pair_r.at[q], device_id=sibling, device_id_type=MESH))
        pairs[q].start()

    lo = pl.ds(0, half)
    hi = pl.ds(half, half)
    ring = {}

    def ring_send(t, index, src, dst, target):
        copy = pltpu.make_async_remote_copy(
            src, dst, ring_s.at[t, index], ring_r.at[t, index], device_id=target, device_id_type=MESH)
        copy.start()
        ring[t, index] = copy

    def merge(t, q):
        if t == 0:
            loads[q].wait()
            pairs[q].wait_recv()
        for c in range(nbc):
            cols = pl.ds(c * block + t * LANES, LANES)
            acc[t, q, c] = loc[q, :, cols] + pair[q, :, cols]

    def ring_one(t):
        merge(t, 0)
        ring_send(t, 0, acc.at[t, 0, lo], first_up.at[t], above)
        ring_send(t, 1, acc.at[t, 0, hi], first_down.at[t], below)
        merge(t, 1)
        ring_send(t, 2, acc.at[t, 1, hi], from_below.at[t, hi], above)
        merge(t, 2)
        ring_send(t, 3, acc.at[t, 2, lo], from_above.at[t, lo], below)
        merge(t, 3)

    def ring_two(t):
        ring[t, 0].wait_recv()
        acc[t, 1, lo] = acc[t, 1, lo] + first_up[t]
        ring_send(t, 4, acc.at[t, 1, lo], from_below.at[t, lo], above)
        ring[t, 1].wait_recv()
        acc[t, 2, hi] = acc[t, 2, hi] + first_down[t]
        ring_send(t, 5, acc.at[t, 2, hi], from_above.at[t, hi], below)

    def ring_end(t):
        for index in range(2, 6):
            ring[t, index].wait_recv()
        gsel[t] = (acc[t, 3] + from_below[t]) + from_above[t]

    p1 = {}

    def exchange_shards(t):
        for k in s_steps:
            target = shard_peer(me_s, k, dims)
            for j in range(CAP):
                send1[t, k, j] = gsel[t, tab[0, o_sends + target * CAP + j]]
            copy = pltpu.make_async_remote_copy(
                send1.at[t, k], recv1[t].at[me_s], p1_s.at[t, k], p1_r.at[t, k],
                device_id=(me_d, target), device_id_type=MESH)
            copy.start()
            p1[t, k] = copy
        for j in range(CAP):
            recv1[t][me_s, j] = gsel[t, tab[0, o_sends + me_s * CAP + j]]

    p2 = {}

    def exchange_dp(t):
        for k in s_steps:
            p1[t, k].wait_recv()
        for k, step in enumerate(z_steps + [(0, 0)]):
            target = dp_peer(me_d, step, ndp)
            place = tab[0, o_rank + target]
            r = place // CAP
            j = place % CAP
            for x in range(nx):
                send2[t, k, x] = recv1[t][r * nx + x, j]
            if k < len(z_steps):
                copy = pltpu.make_async_remote_copy(
                    send2.at[t, k], gblk.at[t, :, me_d], p2_s.at[t, k], p2_r.at[t, k],
                    device_id=(target, me_s), device_id_type=MESH)
            else:
                copy = pltpu.make_async_copy(send2.at[t, k], gblk.at[t, :, me_d], p2_s.at[t, k])
            copy.start()
            p2[t, k] = copy

    def adam_rows(t):
        for c in range(nbc):
            cols = pl.ds(c * block + t * LANES, LANES)
            g = gsel[t, c]
            m = 0.9 * mbuf[:, cols] + 0.1 * g
            v = 0.99 * vbuf[:, cols] + 0.01 * g * g
            mbuf[:, cols] = m
            vbuf[:, cols] = v
            a = m / (jnp.sqrt(v) + 1e-08)
            part = jnp.sum(a * a, axis=0, keepdims=True)
            if t == 0:
                asend[pl.ds(c, 1), :] = part
            else:
                asend[pl.ds(c, 1), :] = asend[pl.ds(c, 1), :] + part

    def shards_out(t):
        ring_end(t)
        exchange_shards(t)

    ring_one(0)
    for t in range(1, chunks):
        ring_one(t)
        if t == 1:
            for copy in lists:
                copy.wait()
            tvec[...] = route_table(ibuf[0], ibuf[1], me_d, me_s, dims)
            table_in = pltpu.make_async_copy(tvec, tab, t_sem.at[0])
            table_in.start()
            table_out = pltpu.make_async_copy(tvec, tab_out, t_sem.at[1])
            table_out.start()
        ring_two(t - 1)
        if t == 1:
            table_in.wait()
        if t >= 2:
            shards_out(t - 2)
    ring_two(chunks - 1)
    m_in.wait()
    v_in.wait()
    sent = 0
    for t in range(max(chunks - 2, 0), chunks):
        if sent < t:
            exchange_dp(sent)
            sent += 1
        shards_out(t)
    done = 0
    while sent < chunks:
        if sent < chunks - 2:
            exchange_dp(sent)
            sent += 1
        for _ in range(2):
            if done < chunks:
                adam_rows(done)
                done += 1
        exchange_dp(sent)
        sent += 1
    while done < chunks:
        adam_rows(done)
        done += 1

    m_out = pltpu.make_async_copy(mbuf, mom_out, io_sem.at[0])
    v_out = pltpu.make_async_copy(vbuf, sec_out, io_sem.at[1])
    a_out = pltpu.make_async_copy(asend, adam_out, io_sem.at[2])
    for copy in (m_out, v_out, a_out):
        copy.start()

    for copy in pairs + list(ring.values()) + list(p1.values()):
        copy.wait_send()
    for (t, k), copy in p2.items():
        if k < len(z_steps):
            copy.wait_send()
            copy.wait_recv()
        else:
            copy.wait()
    m_out.wait()
    v_out.wait()
    a_out.wait()
    table_out.wait()


def shard_peer(me_s, k, dims):
    _, _, nx, nbr, _ = dims
    return (me_s // nx + k // nx) % nbr * nx + (me_s % nx + k % nx) % nx


def forward(own, steps, grad, mom, sec, dims, block):
    ndp, nshard, nx, nbr, nbc = dims
    rows_dev, columns = mom.shape
    chunks = block // LANES
    f32 = jnp.float32
    hbm = pl.BlockSpec(memory_space=pltpu.HBM)
    dma = pltpu.SemaphoreType.DMA
    piece = (rows_dev, LANES)
    return pl.pallas_call(
        functools.partial(forward_kernel, dims, block),
        out_shape=(
            jax.ShapeDtypeStruct((chunks, nx, ndp) + piece, f32),
            jax.ShapeDtypeStruct((rows_dev, columns), f32),
            jax.ShapeDtypeStruct((rows_dev, columns), f32),
            jax.ShapeDtypeStruct((nbc, LANES), f32),
            jax.ShapeDtypeStruct((1, LANES), jnp.int32),
        ),
        in_specs=[hbm] * 5,
        out_specs=(hbm,) * 5,
        scratch_shapes=[
            pltpu.VMEM((2, 1, nbr * nbc), jnp.int32),
            pltpu.VMEM((1, LANES), jnp.int32),
            pltpu.SMEM((1, LANES), jnp.int32),
            pltpu.VMEM((4, rows_dev, columns), f32),
            pltpu.VMEM((4, rows_dev, columns), f32),
            pltpu.VMEM((chunks, 4, nbc) + piece, f32),
            pltpu.VMEM((chunks, nbc // 2) + piece, f32),
            pltpu.VMEM((chunks, nbc // 2) + piece, f32),
            pltpu.VMEM((chunks, nbc) + piece, f32),
            pltpu.VMEM((chunks, nbc) + piece, f32),
            pltpu.VMEM((chunks, nbc) + piece, f32),
            pltpu.VMEM((rows_dev, columns), f32),
            pltpu.VMEM((rows_dev, columns), f32),
            pltpu.VMEM((chunks, nshard, CAP) + piece, f32),
            [pltpu.VMEM((nshard, CAP) + piece, f32) for _ in range(chunks)],
            pltpu.VMEM((chunks, ndp, nx) + piece, f32),
            pltpu.VMEM((nbc, LANES), f32),
            dma((4,)),
            dma((4,)),
            dma((4,)),
            dma((chunks, 6)),
            dma((chunks, 6)),
            dma((chunks, nshard)),
            dma((chunks, nshard)),
            dma((chunks, ndp)),
            dma((chunks, ndp)),
            dma((3,)),
            dma((2,)),
        ],
        compiler_params=pltpu.CompilerParams(
            collective_id=0, has_side_effects=True, vmem_limit_bytes=58 * MIB),
    )(own, steps, grad, mom, sec)


def split(value):
    high = value.astype(jnp.bfloat16)
    low = (value - high.astype(jnp.float32)).astype(jnp.bfloat16)
    return high, low


def dot(left, right, axes=((1,), (0,))):
    return lax.dot_general(left, right, (axes, ((), ())), preferred_element_type=jnp.float32)


def product(first, second_factor):
    return dot(first[0], second_factor[0]) + (
        dot(first[0], second_factor[1]) + dot(first[1], second_factor[0]))


def mirrored(top, corner):
    half = corner.shape[0]
    return jnp.concatenate([top, jnp.concatenate([top[:, half:].T, corner], axis=1)], axis=0)


def gram(value, axes):
    cross = dot(value[0], value[1], axes)
    return dot(value[0], value[0], axes) + (cross + cross.T)


def square_of(value):
    high, low = value
    half = high.shape[0] // 2
    cross = dot(high, low)
    top = dot(high[:half], high) + (
        cross[:half] + jnp.concatenate([cross[:half, :half].T, cross[half:, :half].T], axis=1))
    corner = dot(high[half:], high[:, half:]) + (cross[half:, half:] + cross[half:, half:].T)
    return mirrored(top, corner)


def even_product(first, second_factor):
    half = first[0].shape[0] // 2
    top = product((first[0][:half], first[1][:half]), second_factor)
    corner = product(
        (first[0][half:], first[1][half:]), (second_factor[0][:, half:], second_factor[1][:, half:]))
    return mirrored(top, corner)


def owner_kernel(step_place, tab, gblk, left_prev, right_prev, mom, sec,
                 left_out, right_out, lroot_out, rroot_out, mom_out, sec_out,
                 g_ref, stat, root, mbuf, vbuf, sem, io_sem):
    taken = tab[0, step_place + 1]
    size = g_ref.shape[1]
    g_in = pltpu.make_async_copy(gblk, g_ref, sem.at[0])
    ins = [pltpu.make_async_copy(prev, stat.at[i], sem.at[1 + i])
           for i, prev in enumerate((left_prev, right_prev))]
    g_in.start()
    for copy in ins:
        copy.start()
    moves = [pltpu.make_async_copy(src, dst, io_sem.at[i])
             for i, (src, dst) in enumerate(((mom, mbuf), (sec, vbuf)))]
    for copy in moves:
        copy.start()
    g_in.wait()
    for copy in ins:
        copy.wait()
    for copy in moves:
        copy.wait()
    moves = [pltpu.make_async_copy(src, dst, io_sem.at[i])
             for i, (src, dst) in enumerate(((mbuf, mom_out), (vbuf, sec_out)))]
    for copy in moves:
        copy.start()
    stat_outs = [pltpu.make_async_copy(stat.at[i], out, sem.at[1 + i])
                 for i, out in enumerate((left_out, right_out))]
    root_outs = [pltpu.make_async_copy(root.at[i], out, sem.at[3 + i])
                 for i, out in enumerate((lroot_out, rroot_out))]
    two = range(2)

    @pl.when(taken == 0)
    def _():
        for i in two:
            stat[i] = jnp.zeros((size, size), jnp.float32)
            root[i] = jnp.zeros((size, size), jnp.float32)
            stat_outs[i].start()
            root_outs[i].start()
        for i in two:
            stat_outs[i].wait()
            root_outs[i].wait()

    @pl.when(taken != 0)
    def _():
        diagonal = lax.broadcasted_iota(jnp.int32, (size, size), 0) == lax.broadcasted_iota(
            jnp.int32, (size, size), 1)

        def complement(matrix):
            return split(jnp.where(diagonal, 1.25, 0.0) - 0.25 * matrix)

        g = split(joined(g_ref))
        grams = [gram(g, axes) for axes in (((1,), (1,)), ((0,), (0,)))]
        for i in two:
            stat[i] = 0.95 * stat[i] + grams[i]
            stat_outs[i].start()
        scales, matrix = [], []
        for i in two:
            shifted = stat[i] + jnp.where(diagonal, 0.0001, 0.0)
            scale = 2.5 / jnp.sqrt(jnp.full((1, 1), jnp.sum(shifted * shifted)))
            scales.append(jnp.sqrt(jnp.sqrt(scale)))
            matrix.append(scale * shifted)
        factor = [complement(matrix[i]) for i in two]
        square = [split(square_of(factor[i])) for i in two]
        fourth = [split(square_of(square[i])) for i in two]
        matrix = [even_product(fourth[i], split(matrix[i])) for i in two]
        after = [complement(matrix[i]) for i in two]
        square = [split(square_of(after[i])) for i in two]
        current = [even_product(factor[i], after[i]) for i in two]
        fourth = [split(square_of(square[i])) for i in two]
        matrix = [even_product(fourth[i], split(matrix[i])) for i in two]
        more = tab[0, step_place] > 2
        for i in two:
            third = even_product(split(current[i]), complement(matrix[i]))
            root[i] = scales[i] * jnp.where(more, third, current[i])
            root_outs[i].start()
        for i in two:
            stat_outs[i].wait()
            root_outs[i].wait()

    for copy in moves:
        copy.wait()


def owner_step(tab, gblk, left_prev, right_prev, mom, sec, step_place):
    size = gblk.shape[1]
    f32 = jnp.float32
    square = jax.ShapeDtypeStruct((size, size), f32)
    rows = jax.ShapeDtypeStruct(mom.shape, f32)
    hbm = pl.BlockSpec(memory_space=pltpu.HBM)
    return pl.pallas_call(
        functools.partial(owner_kernel, step_place),
        out_shape=(square,) * 4 + (rows,) * 2,
        in_specs=[pl.BlockSpec(memory_space=pltpu.SMEM)] + [hbm] * 5,
        out_specs=(hbm,) * 6,
        scratch_shapes=[
            pltpu.VMEM(gblk.shape, f32),
            pltpu.VMEM((2, size, size), f32),
            pltpu.VMEM((2, size, size), f32),
            pltpu.VMEM(mom.shape, f32),
            pltpu.VMEM(mom.shape, f32),
            pltpu.SemaphoreType.DMA((5,)),
            pltpu.SemaphoreType.DMA((2,)),
        ],
        compiler_params=pltpu.CompilerParams(vmem_limit_bytes=58 * MIB),
        cost_estimate=pl.CostEstimate(
            flops=100 * size ** 3, bytes_accessed=36 * size * size, transcendentals=0),
    )(tab, gblk, left_prev, right_prev, mom, sec)


def back_kernel(dims, block, rows_dev, tab, gblk, lroot, rroot, adam, update,
                gbuf, lbuf, rbuf, pbuf, recv2, send1, recv1, out, asend, arecv, xsend, xrecv,
                p2_s, p2_r, a_s, a_r, x_s, x_r, p1_s, p1_r, io_sem):
    ndp, nshard, nx, nbr, nbc = dims
    _, _, o_row, o_final, _ = offsets(dims)
    chunks = block // LANES
    me_d = lax.axis_index("dp")
    me_s = lax.axis_index("shard")
    ins = [pltpu.make_async_copy(src, dst, io_sem.at[i])
           for i, (src, dst) in enumerate(((lroot, lbuf), (gblk, gbuf), (rroot, rbuf), (adam, asend)))]
    for copy in ins:
        copy.start()
    z_steps = dp_steps(ndp)
    s_steps = far_first(nshard, nx)
    peers = [(dp_peer(me_d, step, ndp), me_s) for step in z_steps] + [
        (me_d, shard_peer(me_s, k, dims)) for k in s_steps]
    signal(peers)
    for copy in ins:
        copy.wait()
    turned = split(product(split(lbuf[...]), split(joined(gbuf))))
    way = product(turned, split(rbuf[...]))
    power = jnp.sum(jnp.sum(way * way, axis=0, keepdims=True), axis=1, keepdims=True)
    way = way * (1.0 / jnp.sqrt(power + 1e-12))
    for t in range(chunks):
        for x in range(nx):
            for d in range(ndp):
                top = (x * ndp + d) * rows_dev
                pbuf[t, d, x] = way[top:top + rows_dev, t * LANES:(t + 1) * LANES]
    await_peers(peers)

    acopies = []
    for k, step in enumerate(z_steps):
        copy = pltpu.make_async_remote_copy(
            asend, arecv.at[k], a_s.at[k], a_r.at[k],
            device_id=(dp_peer(me_d, step, ndp), me_s), device_id_type=MESH)
        copy.start()
        acopies.append(copy)
    p2 = {}
    for t in range(chunks):
        for k, step in enumerate(z_steps):
            target = dp_peer(me_d, step, ndp)
            copy = pltpu.make_async_remote_copy(
                pbuf.at[t, target], recv2[t].at[me_d], p2_s.at[t, k], p2_r.at[t, k],
                device_id=(target, me_s), device_id_type=MESH)
            copy.start()
            p2[t, k] = copy
        recv2[t][me_d] = pbuf[t, me_d]
    total = asend[...]
    for k, copy in enumerate(acopies):
        copy.wait_recv()
        total = total + arecv[k]
    xsend[...] = total
    xcopies = []
    for k in range(1, nx):
        copy = pltpu.make_async_remote_copy(
            xsend, xrecv.at[k], x_s.at[k], x_r.at[k],
            device_id=(me_d, me_s // nx * nx + (me_s % nx + k) % nx), device_id_type=MESH)
        copy.start()
        xcopies.append(copy)

    p1 = {}
    for t in range(chunks):
        for k in range(len(z_steps)):
            p2[t, k].wait_recv()

        def wanted(target, j):
            rank = tab[0, o_row + target // nx * CAP + j]
            return recv2[t][rank, target % nx]

        for k in s_steps:
            target = shard_peer(me_s, k, dims)
            for j in range(CAP):
                send1[t, k, j] = wanted(target, j)
            copy = pltpu.make_async_remote_copy(
                send1.at[t, k], recv1[t].at[pl.ds(me_s * CAP, CAP)], p1_s.at[t, k], p1_r.at[t, k],
                device_id=(me_d, target), device_id_type=MESH)
            copy.start()
            p1[t, k] = copy
        for j in range(CAP):
            recv1[t][me_s * CAP + j] = wanted(me_s, j)
    for k in range(1, nx):
        xcopies[k - 1].wait_recv()
        total = total + xrecv[k]
    ad = jnp.broadcast_to(jnp.sqrt(jnp.sum(total, axis=1, keepdims=True)), total.shape)
    for t in range(chunks):
        for k in s_steps:
            p1[t, k].wait_recv()
        for c in range(nbc):
            cols = pl.ds(c * block + t * LANES, LANES)
            out[:, cols] = recv1[t][tab[0, o_final + c]] * ad[c:c + 1, :]
    done = pltpu.make_async_copy(out, update, io_sem.at[0])
    done.start()
    for copy in list(p2.values()) + acopies + xcopies + list(p1.values()):
        copy.wait_send()
    done.wait()


def back(tab, gblk, lroot, rroot, adam, dims, block, rows_dev, columns):
    ndp, nshard, nx, nbr, nbc = dims
    chunks = block // LANES
    f32 = jnp.float32
    hbm = pl.BlockSpec(memory_space=pltpu.HBM)
    dma = pltpu.SemaphoreType.DMA
    piece = (rows_dev, LANES)
    return pl.pallas_call(
        functools.partial(back_kernel, dims, block, rows_dev),
        out_shape=jax.ShapeDtypeStruct((rows_dev, columns), f32),
        in_specs=[pl.BlockSpec(memory_space=pltpu.SMEM)] + [hbm] * 4,
        out_specs=pl.BlockSpec(memory_space=pl.ANY),
        scratch_shapes=[
            pltpu.VMEM(gblk.shape, f32),
            pltpu.VMEM((block, block), f32),
            pltpu.VMEM((block, block), f32),
            pltpu.VMEM((chunks, ndp, nx) + piece, f32),
            [pltpu.VMEM((ndp, nx) + piece, f32) for _ in range(chunks)],
            pltpu.VMEM((chunks, nshard, CAP) + piece, f32),
            [pltpu.VMEM((nshard * CAP,) + piece, f32) for _ in range(chunks)],
            pltpu.VMEM((rows_dev, columns), f32),
            pltpu.VMEM((nbc, LANES), f32),
            pltpu.VMEM((ndp, nbc, LANES), f32),
            pltpu.VMEM((nbc, LANES), f32),
            pltpu.VMEM((nx, nbc, LANES), f32),
            dma((chunks, ndp)),
            dma((chunks, ndp)),
            dma((ndp,)),
            dma((ndp,)),
            dma((nx,)),
            dma((nx,)),
            dma((chunks, nshard)),
            dma((chunks, nshard)),
            dma((4,)),
        ],
        compiler_params=pltpu.CompilerParams(
            collective_id=1, has_side_effects=True, vmem_limit_bytes=53 * MIB),
    )(tab, gblk, lroot, rroot, adam)


def local(grad_parts, moment, second, left_prev, right_prev, owners, newton_steps):
    ndp = lax.axis_size("dp")
    nshard = lax.axis_size("shard")
    _, rows_dev, columns = moment.shape
    block = left_prev.shape[-1]
    nx = block // (rows_dev * ndp)
    dims = (ndp, nshard, nx, nshard // nx, columns // block)
    gblk, mom, sec, adam, tab = forward(
        owners[None], newton_steps[None], grad_parts[0], moment[0], second[0], dims, block)
    gblk = gblk.reshape(block // LANES, block, LANES)
    left, right, lroot, rroot, mom, sec = owner_step(
        tab, gblk, left_prev[0, 0, 0], right_prev[0, 0, 0], mom, sec, offsets(dims)[4])
    update = back(tab, gblk, lroot, rroot, adam, dims, block, rows_dev, columns)
    slots = (1, 1, 1, block, block)
    return (
        update[None],
        mom[None],
        sec[None],
        left.reshape(slots),
        right.reshape(slots),
        lroot.reshape(slots),
        rroot.reshape(slots),
    )


def solution(mesh):
    rows = P("shard", "dp", None)
    slots = P("dp", "shard", None, None, None)
    return jax.shard_map(
        local,
        mesh=mesh,
        in_specs=(P("dp", "shard", None), rows, rows, slots, slots, P(), P()),
        out_specs=(rows, rows, rows, slots, slots, slots, slots),
        check_vma=False,
    )
```

```python
import functools

import jax
import jax.numpy as jnp
from jax import lax
from jax.experimental import pallas as pl
from jax.experimental.pallas import tpu as pltpu
from jax.sharding import PartitionSpec as P

MESH = pl.DeviceIdType.MESH
CORES = 2
LANES = 128
CAP = 2
MIB = 1 << 20


def route_table(own, steps, my_dp, my_shard, dims):
    ndp, nshard, nx, nbr, nbc = dims
    count = nbr * nbc
    o_sends, o_rank, o_row, o_final, o_steps = offsets(dims)
    down = lax.broadcasted_iota(jnp.int32, (count, count), 0)
    across = lax.broadcasted_iota(jnp.int32, (count, count), 1)
    wide = jnp.broadcast_to(own, (count, count))

    def turned(row):
        return jnp.sum(jnp.where(down == across, jnp.broadcast_to(row, (count, count)), 0), axis=1, keepdims=True)

    owner = turned(own)
    earlier = jnp.where((owner == wide) & (across < down), 1, 0)
    rank = jnp.sum(earlier, axis=1, keepdims=True)
    sub = jnp.sum(jnp.where(across // nbc == down // nbc, earlier, 0), axis=1, keepdims=True)
    count_of = turned(steps)
    lane = lax.broadcasted_iota(jnp.int32, (count, 128), 1)
    block = lax.broadcasted_iota(jnp.int32, (count, 128), 0)

    def spread(column):
        return jnp.broadcast_to(column, (count, 128))

    owner, rank, sub, count_of = (spread(column) for column in (owner, rank, sub, count_of))
    row, column = block // nbc, block % nbc
    mine = jnp.where(owner == my_shard, 1, 0)
    here = jnp.where(row == my_shard // nx, 1, 0)
    slot = owner * CAP + sub
    place = row * CAP + sub
    key = jnp.where(lane < o_rank, slot, jnp.where(lane < o_row, rank + o_rank, jnp.where(
        lane < o_final, place + o_row, jnp.where(lane < o_steps, column + o_final, -1))))
    value = jnp.where(lane < o_rank, column, jnp.where(lane < o_row, place, jnp.where(
        lane < o_final, rank, slot)))
    chosen = jnp.where((lane < o_rank) | (lane >= o_final), here, mine)
    table = jnp.where(key == lane, value * chosen, 0)
    held = jnp.where(rank == my_dp, mine, 0)
    table = table + jnp.where(lane == o_steps, held * count_of, jnp.where(lane == o_steps + 1, held, 0))
    return jnp.sum(table, axis=0, keepdims=True)


def offsets(dims):
    ndp, nshard, nx, nbr, nbc = dims
    sends = 0
    by_rank = sends + nshard * CAP
    by_row = by_rank + ndp
    finals = by_row + nbr * CAP
    steps = finals + nbc
    return sends, by_rank, by_row, finals, steps


def signal(peers):
    barrier = pltpu.get_barrier_semaphore()
    for peer in peers:
        pl.semaphore_signal(barrier, inc=1, device_id=peer, device_id_type=MESH)


def await_peers(peers):
    pl.semaphore_wait(pltpu.get_barrier_semaphore(), len(peers))


def greet(peers):
    signal(peers)
    await_peers(peers)


def joined(chunked):
    return jnp.concatenate([chunked[t] for t in range(chunked.shape[0])], axis=1)


def far_first(count, width):
    def length(k):
        across, down = k % width, k // width
        high = count // width
        return min(across, width - across) + min(down, high - down)

    return sorted(range(1, count), key=lambda k: -length(k))


def dp_steps(ndp):
    nz = ndp // CORES
    steps = [(a, c) for a in range(nz) for c in range(CORES) if a or c]
    return sorted(steps, key=lambda k: -min(k[0], nz - k[0]))


def dp_peer(me_d, step, ndp):
    nz = ndp // CORES
    return (me_d // CORES + step[0]) % nz * CORES + (me_d % CORES + step[1]) % CORES


def forward_kernel(dims, block, own, steps, grad, mom, sec,
                   gblk, mom_out, sec_out, adam_out, tab_out,
                   ibuf, tvec, tab, loc, pair, other, raw, crossed, acc, first_up, first_down, from_below, from_above,
                   gsel, mbuf, vbuf, send1, recv1, send2, asend,
                   loc_sem, pair_s, pair_r, cross_s, cross_r, ring_s, ring_r, p1_s, p1_r, p2_s, p2_r,
                   io_sem, t_sem):
    ndp, nshard, nx, nbr, nbc = dims
    o_sends, o_rank, _, _, _ = offsets(dims)
    nz = ndp // CORES
    chunks = block // LANES
    half = nbc // 2
    rows_dev = mom.shape[0]
    me_d = lax.axis_index("dp")
    me_s = lax.axis_index("shard")
    z = me_d // CORES
    core = me_d % CORES

    def zed(step):
        return (z + step) % nz

    def rows_of(zz, cc):
        return pl.ds(pl.multiple_of((zz * CORES + cc) * rows_dev, rows_dev), rows_dev)

    order = (2, 1, nz - 1, 0)
    loads = []
    lists = [pltpu.make_async_copy(src, ibuf.at[i], t_sem.at[i]) for i, src in enumerate((own, steps))]
    for copy in lists:
        copy.start()
    for q, step in enumerate(order):
        loads.append(pltpu.make_async_copy(
            grad.at[rows_of(zed(step), core), :], loc.at[q], loc_sem.at[q]))
    other_in = pltpu.make_async_copy(grad.at[rows_of(zed(order[0]), 1 - core), :], other, t_sem.at[2])
    loads[0].start()
    other_in.start()
    m_in = pltpu.make_async_copy(mom, mbuf, io_sem.at[0])
    v_in = pltpu.make_async_copy(sec, vbuf, io_sem.at[1])

    z_steps = dp_steps(ndp)
    s_steps = far_first(nshard, nx)
    greet([(dp_peer(me_d, step, ndp), me_s) for step in reversed(z_steps)]
          + [(me_d, shard_peer(me_s, k, dims)) for k in s_steps])

    sibling = (z * CORES + (1 - core), me_s)
    above = (zed(1) * CORES + core, me_s)
    below = (zed(nz - 1) * CORES + core, me_s)
    pairs = []
    for q, step in enumerate(order):
        pairs.append(pltpu.make_async_remote_copy(
            grad.at[rows_of(zed(step), 1 - core), :], pair.at[q],
            pair_s.at[q], pair_r.at[q], device_id=sibling, device_id_type=MESH))
    pairs[0].start()
    for load in loads[1:]:
        load.start()

    lo = pl.ds(0, half)
    hi = pl.ds(half, half)
    ring = {}
    cross = []

    def ring_send(t, index, src, dst, target):
        copy = pltpu.make_async_remote_copy(
            src, dst, ring_s.at[t, index], ring_r.at[t, index], device_id=target, device_id_type=MESH)
        copy.start()
        ring[t, index] = copy

    def merge(t, q):
        if t == (1 if q == 0 else 0):
            if q:
                loads[q].wait()
            pairs[q].wait_recv()
        for c in range(nbc):
            cols = pl.ds(c * block + t * LANES, LANES)
            acc[t, q, c] = loc[q, :, cols] + pair[q, :, cols]

    def ring_raw():
        loads[0].wait()
        other_in.wait()
        for c in range(nbc):
            cols = pl.ds(c * block, LANES)
            acc[0, 0, c] = loc[0, :, cols]
            raw[c] = other[:, cols]
        ring_send(0, 0, acc.at[0, 0, lo], first_up.at[0], above)
        ring_send(0, 1, acc.at[0, 0, hi], first_down.at[0], below)
        for index, (part, target) in enumerate(((lo, above), (hi, below))):
            copy = pltpu.make_async_remote_copy(
                raw.at[part], crossed.at[index], cross_s.at[index], cross_r.at[index],
                device_id=(target[0] + 1 - 2 * core, me_s), device_id_type=MESH)
            copy.start()
            cross.append(copy)

    def ring_far(t):
        merge(t, 0)
        ring_send(t, 0, acc.at[t, 0, lo], first_up.at[t], above)
        ring_send(t, 1, acc.at[t, 0, hi], first_down.at[t], below)

    def ring_one(t):
        merge(t, 1)
        ring_send(t, 2, acc.at[t, 1, hi], from_below.at[t, hi], above)
        merge(t, 2)
        ring_send(t, 3, acc.at[t, 2, lo], from_above.at[t, lo], below)
        merge(t, 3)

    def ring_two(t):
        ring[t, 0].wait_recv()
        if t == 0:
            cross[0].wait_recv()
            first_up[0] = first_up[0] + crossed[0]
        acc[t, 1, lo] = acc[t, 1, lo] + first_up[t]
        ring_send(t, 4, acc.at[t, 1, lo], from_below.at[t, lo], above)
        ring[t, 1].wait_recv()
        if t == 0:
            cross[1].wait_recv()
            first_down[0] = first_down[0] + crossed[1]
        acc[t, 2, hi] = acc[t, 2, hi] + first_down[t]
        ring_send(t, 5, acc.at[t, 2, hi], from_above.at[t, hi], below)

    def ring_end(t):
        for index in range(2, 6):
            ring[t, index].wait_recv()
        gsel[t] = (acc[t, 3] + from_below[t]) + from_above[t]

    p1 = {}

    def exchange_shards(t):
        for k in s_steps:
            target = shard_peer(me_s, k, dims)
            for j in range(CAP):
                send1[t, k, j] = gsel[t, tab[0, o_sends + target * CAP + j]]
            copy = pltpu.make_async_remote_copy(
                send1.at[t, k], recv1[t].at[me_s], p1_s.at[t, k], p1_r.at[t, k],
                device_id=(me_d, target), device_id_type=MESH)
            copy.start()
            p1[t, k] = copy
        for j in range(CAP):
            recv1[t][me_s, j] = gsel[t, tab[0, o_sends + me_s * CAP + j]]

    p2 = {}

    def exchange_dp(t):
        for k in s_steps:
            p1[t, k].wait_recv()
        for k, step in enumerate(z_steps + [(0, 0)]):
            target = dp_peer(me_d, step, ndp)
            place = tab[0, o_rank + target]
            r = place // CAP
            j = place % CAP
            for x in range(nx):
                send2[t, k, x] = recv1[t][r * nx + x, j]
            if k < len(z_steps):
                copy = pltpu.make_async_remote_copy(
                    send2.at[t, k], gblk.at[t, :, me_d], p2_s.at[t, k], p2_r.at[t, k],
                    device_id=(target, me_s), device_id_type=MESH)
            else:
                copy = pltpu.make_async_copy(send2.at[t, k], gblk.at[t, :, me_d], p2_s.at[t, k])
            copy.start()
            p2[t, k] = copy

    def adam_rows(t):
        for c in range(nbc):
            cols = pl.ds(c * block + t * LANES, LANES)
            g = gsel[t, c]
            m = 0.9 * mbuf[:, cols] + 0.1 * g
            v = 0.99 * vbuf[:, cols] + 0.01 * g * g
            mbuf[:, cols] = m
            vbuf[:, cols] = v
            a = m / (jnp.sqrt(v) + 1e-08)
            part = jnp.sum(a * a, axis=0, keepdims=True)
            if t == 0:
                asend[pl.ds(c, 1), :] = part
            else:
                asend[pl.ds(c, 1), :] = asend[pl.ds(c, 1), :] + part

    def shards_out(t):
        ring_end(t)
        exchange_shards(t)

    ring_raw()
    for copy in pairs[1:]:
        copy.start()
    m_in.start()
    v_in.start()
    ring_far(1)
    ring_one(0)
    for t in range(1, chunks):
        if t > 1:
            ring_far(t)
        ring_one(t)
        if t == 1:
            for copy in lists:
                copy.wait()
            tvec[...] = route_table(ibuf[0], ibuf[1], me_d, me_s, dims)
            table_in = pltpu.make_async_copy(tvec, tab, t_sem.at[0])
            table_in.start()
            table_out = pltpu.make_async_copy(tvec, tab_out, t_sem.at[1])
            table_out.start()
        ring_two(t - 1)
        if t == 1:
            table_in.wait()
        if t >= 2:
            shards_out(t - 2)
    ring_two(chunks - 1)
    m_in.wait()
    v_in.wait()
    sent = 0
    for t in range(max(chunks - 2, 0), chunks):
        if sent < t:
            exchange_dp(sent)
            sent += 1
        shards_out(t)
    done = 0
    while sent < chunks:
        if sent < chunks - 2:
            exchange_dp(sent)
            sent += 1
        for _ in range(2):
            if done < chunks:
                adam_rows(done)
                done += 1
        exchange_dp(sent)
        sent += 1
    while done < chunks:
        adam_rows(done)
        done += 1

    m_out = pltpu.make_async_copy(mbuf, mom_out, io_sem.at[0])
    v_out = pltpu.make_async_copy(vbuf, sec_out, io_sem.at[1])
    a_out = pltpu.make_async_copy(asend, adam_out, io_sem.at[2])
    for copy in (m_out, v_out, a_out):
        copy.start()

    for copy in pairs + cross + list(ring.values()) + list(p1.values()):
        copy.wait_send()
    for (t, k), copy in p2.items():
        if k < len(z_steps):
            copy.wait_send()
            copy.wait_recv()
        else:
            copy.wait()
    m_out.wait()
    v_out.wait()
    a_out.wait()
    table_out.wait()


def shard_peer(me_s, k, dims):
    _, _, nx, nbr, _ = dims
    return (me_s // nx + k // nx) % nbr * nx + (me_s % nx + k % nx) % nx


def forward(own, steps, grad, mom, sec, dims, block):
    ndp, nshard, nx, nbr, nbc = dims
    rows_dev, columns = mom.shape
    chunks = block // LANES
    f32 = jnp.float32
    hbm = pl.BlockSpec(memory_space=pltpu.HBM)
    dma = pltpu.SemaphoreType.DMA
    piece = (rows_dev, LANES)
    return pl.pallas_call(
        functools.partial(forward_kernel, dims, block),
        out_shape=(
            jax.ShapeDtypeStruct((chunks, nx, ndp) + piece, f32),
            jax.ShapeDtypeStruct((rows_dev, columns), f32),
            jax.ShapeDtypeStruct((rows_dev, columns), f32),
            jax.ShapeDtypeStruct((nbc, LANES), f32),
            jax.ShapeDtypeStruct((1, LANES), jnp.int32),
        ),
        in_specs=[hbm] * 5,
        out_specs=(hbm,) * 5,
        scratch_shapes=[
            pltpu.VMEM((2, 1, nbr * nbc), jnp.int32),
            pltpu.VMEM((1, LANES), jnp.int32),
            pltpu.SMEM((1, LANES), jnp.int32),
            pltpu.VMEM((4, rows_dev, columns), f32),
            pltpu.VMEM((4, rows_dev, columns), f32),
            pltpu.VMEM((rows_dev, columns), f32),
            pltpu.VMEM((nbc,) + piece, f32),
            pltpu.VMEM((2, nbc // 2) + piece, f32),
            pltpu.VMEM((chunks, 4, nbc) + piece, f32),
            pltpu.VMEM((chunks, nbc // 2) + piece, f32),
            pltpu.VMEM((chunks, nbc // 2) + piece, f32),
            pltpu.VMEM((chunks, nbc) + piece, f32),
            pltpu.VMEM((chunks, nbc) + piece, f32),
            pltpu.VMEM((chunks, nbc) + piece, f32),
            pltpu.VMEM((rows_dev, columns), f32),
            pltpu.VMEM((rows_dev, columns), f32),
            pltpu.VMEM((chunks, nshard, CAP) + piece, f32),
            [pltpu.VMEM((nshard, CAP) + piece, f32) for _ in range(chunks)],
            pltpu.VMEM((chunks, ndp, nx) + piece, f32),
            pltpu.VMEM((nbc, LANES), f32),
            dma((4,)),
            dma((4,)),
            dma((4,)),
            dma((2,)),
            dma((2,)),
            dma((chunks, 6)),
            dma((chunks, 6)),
            dma((chunks, nshard)),
            dma((chunks, nshard)),
            dma((chunks, ndp)),
            dma((chunks, ndp)),
            dma((3,)),
            dma((3,)),
        ],
        compiler_params=pltpu.CompilerParams(
            collective_id=0, has_side_effects=True, vmem_limit_bytes=58 * MIB),
    )(own, steps, grad, mom, sec)


def split(value):
    high = value.astype(jnp.bfloat16)
    low = (value - high.astype(jnp.float32)).astype(jnp.bfloat16)
    return high, low


def dot(left, right, axes=((1,), (0,))):
    return lax.dot_general(left, right, (axes, ((), ())), preferred_element_type=jnp.float32)


def product(first, second_factor):
    return dot(first[0], second_factor[0]) + (
        dot(first[0], second_factor[1]) + dot(first[1], second_factor[0]))


def mirrored(top, corner):
    half = corner.shape[0]
    return jnp.concatenate([top, jnp.concatenate([top[:, half:].T, corner], axis=1)], axis=0)


def gram(value, axes):
    cross = dot(value[0], value[1], axes)
    return dot(value[0], value[0], axes) + (cross + cross.T)


def square_of(value):
    high, low = value
    half = high.shape[0] // 2
    cross = dot(high, low)
    top = dot(high[:half], high) + (
        cross[:half] + jnp.concatenate([cross[:half, :half].T, cross[half:, :half].T], axis=1))
    corner = dot(high[half:], high[:, half:]) + (cross[half:, half:] + cross[half:, half:].T)
    return mirrored(top, corner)


def even_product(first, second_factor):
    half = first[0].shape[0] // 2
    top = product((first[0][:half], first[1][:half]), second_factor)
    corner = product(
        (first[0][half:], first[1][half:]), (second_factor[0][:, half:], second_factor[1][:, half:]))
    return mirrored(top, corner)


def owner_kernel(step_place, tab, gblk, left_prev, right_prev, mom, sec,
                 left_out, right_out, lroot_out, rroot_out, mom_out, sec_out,
                 g_ref, stat, root, mbuf, vbuf, sem, io_sem):
    taken = tab[0, step_place + 1]
    size = g_ref.shape[1]
    g_in = pltpu.make_async_copy(gblk, g_ref, sem.at[0])
    ins = [pltpu.make_async_copy(prev, stat.at[i], sem.at[1 + i])
           for i, prev in enumerate((left_prev, right_prev))]
    g_in.start()
    for copy in ins:
        copy.start()
    moves = [pltpu.make_async_copy(src, dst, io_sem.at[i])
             for i, (src, dst) in enumerate(((mom, mbuf), (sec, vbuf)))]
    for copy in moves:
        copy.start()
    g_in.wait()
    for copy in ins:
        copy.wait()
    for copy in moves:
        copy.wait()
    moves = [pltpu.make_async_copy(src, dst, io_sem.at[i])
             for i, (src, dst) in enumerate(((mbuf, mom_out), (vbuf, sec_out)))]
    for copy in moves:
        copy.start()
    stat_outs = [pltpu.make_async_copy(stat.at[i], out, sem.at[1 + i])
                 for i, out in enumerate((left_out, right_out))]
    root_outs = [pltpu.make_async_copy(root.at[i], out, sem.at[3 + i])
                 for i, out in enumerate((lroot_out, rroot_out))]
    two = range(2)

    @pl.when(taken == 0)
    def _():
        for i in two:
            stat[i] = jnp.zeros((size, size), jnp.float32)
            root[i] = jnp.zeros((size, size), jnp.float32)
            stat_outs[i].start()
            root_outs[i].start()
        for i in two:
            stat_outs[i].wait()
            root_outs[i].wait()

    @pl.when(taken != 0)
    def _():
        diagonal = lax.broadcasted_iota(jnp.int32, (size, size), 0) == lax.broadcasted_iota(
            jnp.int32, (size, size), 1)

        def complement(matrix):
            return split(jnp.where(diagonal, 1.25, 0.0) - 0.25 * matrix)

        g = split(joined(g_ref))
        grams = [gram(g, axes) for axes in (((1,), (1,)), ((0,), (0,)))]
        for i in two:
            stat[i] = 0.95 * stat[i] + grams[i]
            stat_outs[i].start()
        scales, matrix = [], []
        for i in two:
            shifted = stat[i] + jnp.where(diagonal, 0.0001, 0.0)
            scale = 2.5 / jnp.sqrt(jnp.full((1, 1), jnp.sum(shifted * shifted)))
            scales.append(jnp.sqrt(jnp.sqrt(scale)))
            matrix.append(scale * shifted)
        factor = [complement(matrix[i]) for i in two]
        square = [split(square_of(factor[i])) for i in two]
        fourth = [split(square_of(square[i])) for i in two]
        matrix = [even_product(fourth[i], split(matrix[i])) for i in two]
        after = [complement(matrix[i]) for i in two]
        square = [split(square_of(after[i])) for i in two]
        current = [even_product(factor[i], after[i]) for i in two]
        fourth = [split(square_of(square[i])) for i in two]
        matrix = [even_product(fourth[i], split(matrix[i])) for i in two]
        more = tab[0, step_place] > 2
        for i in two:
            third = even_product(split(current[i]), complement(matrix[i]))
            root[i] = scales[i] * jnp.where(more, third, current[i])
            root_outs[i].start()
        for i in two:
            stat_outs[i].wait()
            root_outs[i].wait()

    for copy in moves:
        copy.wait()


def owner_step(tab, gblk, left_prev, right_prev, mom, sec, step_place):
    size = gblk.shape[1]
    f32 = jnp.float32
    square = jax.ShapeDtypeStruct((size, size), f32)
    rows = jax.ShapeDtypeStruct(mom.shape, f32)
    hbm = pl.BlockSpec(memory_space=pltpu.HBM)
    return pl.pallas_call(
        functools.partial(owner_kernel, step_place),
        out_shape=(square,) * 4 + (rows,) * 2,
        in_specs=[pl.BlockSpec(memory_space=pltpu.SMEM)] + [hbm] * 5,
        out_specs=(hbm,) * 6,
        scratch_shapes=[
            pltpu.VMEM(gblk.shape, f32),
            pltpu.VMEM((2, size, size), f32),
            pltpu.VMEM((2, size, size), f32),
            pltpu.VMEM(mom.shape, f32),
            pltpu.VMEM(mom.shape, f32),
            pltpu.SemaphoreType.DMA((5,)),
            pltpu.SemaphoreType.DMA((2,)),
        ],
        compiler_params=pltpu.CompilerParams(vmem_limit_bytes=58 * MIB),
        cost_estimate=pl.CostEstimate(
            flops=100 * size ** 3, bytes_accessed=36 * size * size, transcendentals=0),
    )(tab, gblk, left_prev, right_prev, mom, sec)


def back_kernel(dims, block, rows_dev, tab, gblk, lroot, rroot, adam, update,
                gbuf, lbuf, rbuf, pbuf, recv2, send1, recv1, out, asend, arecv, xsend, xrecv,
                p2_s, p2_r, a_s, a_r, x_s, x_r, p1_s, p1_r, io_sem):
    ndp, nshard, nx, nbr, nbc = dims
    _, _, o_row, o_final, _ = offsets(dims)
    chunks = block // LANES
    me_d = lax.axis_index("dp")
    me_s = lax.axis_index("shard")
    ins = [pltpu.make_async_copy(src, dst, io_sem.at[i])
           for i, (src, dst) in enumerate(((lroot, lbuf), (gblk, gbuf), (rroot, rbuf), (adam, asend)))]
    for copy in ins:
        copy.start()
    z_steps = dp_steps(ndp)
    s_steps = far_first(nshard, nx)
    peers = [(dp_peer(me_d, step, ndp), me_s) for step in z_steps] + [
        (me_d, shard_peer(me_s, k, dims)) for k in s_steps]
    signal(peers)
    for copy in ins:
        copy.wait()
    turned = split(product(split(lbuf[...]), split(joined(gbuf))))
    way = product(turned, split(rbuf[...]))
    power = jnp.sum(jnp.sum(way * way, axis=0, keepdims=True), axis=1, keepdims=True)
    way = way * (1.0 / jnp.sqrt(power + 1e-12))
    for t in range(chunks):
        for x in range(nx):
            for d in range(ndp):
                top = (x * ndp + d) * rows_dev
                pbuf[t, d, x] = way[top:top + rows_dev, t * LANES:(t + 1) * LANES]
    await_peers(peers)

    acopies = []
    for k, step in enumerate(z_steps):
        copy = pltpu.make_async_remote_copy(
            asend, arecv.at[k], a_s.at[k], a_r.at[k],
            device_id=(dp_peer(me_d, step, ndp), me_s), device_id_type=MESH)
        copy.start()
        acopies.append(copy)
    p2 = {}
    for t in range(chunks):
        for k, step in enumerate(z_steps):
            target = dp_peer(me_d, step, ndp)
            copy = pltpu.make_async_remote_copy(
                pbuf.at[t, target], recv2[t].at[me_d], p2_s.at[t, k], p2_r.at[t, k],
                device_id=(target, me_s), device_id_type=MESH)
            copy.start()
            p2[t, k] = copy
        recv2[t][me_d] = pbuf[t, me_d]
    total = asend[...]
    for k, copy in enumerate(acopies):
        copy.wait_recv()
        total = total + arecv[k]
    xsend[...] = total
    xcopies = []
    for k in range(1, nx):
        copy = pltpu.make_async_remote_copy(
            xsend, xrecv.at[k], x_s.at[k], x_r.at[k],
            device_id=(me_d, me_s // nx * nx + (me_s % nx + k) % nx), device_id_type=MESH)
        copy.start()
        xcopies.append(copy)

    p1 = {}
    for t in range(chunks):
        for k in range(len(z_steps)):
            p2[t, k].wait_recv()

        def wanted(target, j):
            rank = tab[0, o_row + target // nx * CAP + j]
            return recv2[t][rank, target % nx]

        for k in s_steps:
            target = shard_peer(me_s, k, dims)
            for j in range(CAP):
                send1[t, k, j] = wanted(target, j)
            copy = pltpu.make_async_remote_copy(
                send1.at[t, k], recv1[t].at[pl.ds(me_s * CAP, CAP)], p1_s.at[t, k], p1_r.at[t, k],
                device_id=(me_d, target), device_id_type=MESH)
            copy.start()
            p1[t, k] = copy
        for j in range(CAP):
            recv1[t][me_s * CAP + j] = wanted(me_s, j)
    for k in range(1, nx):
        xcopies[k - 1].wait_recv()
        total = total + xrecv[k]
    ad = jnp.broadcast_to(jnp.sqrt(jnp.sum(total, axis=1, keepdims=True)), total.shape)
    for t in range(chunks):
        for k in s_steps:
            p1[t, k].wait_recv()
        for c in range(nbc):
            cols = pl.ds(c * block + t * LANES, LANES)
            out[:, cols] = recv1[t][tab[0, o_final + c]] * ad[c:c + 1, :]
    done = pltpu.make_async_copy(out, update, io_sem.at[0])
    done.start()
    for copy in list(p2.values()) + acopies + xcopies + list(p1.values()):
        copy.wait_send()
    done.wait()


def back(tab, gblk, lroot, rroot, adam, dims, block, rows_dev, columns):
    ndp, nshard, nx, nbr, nbc = dims
    chunks = block // LANES
    f32 = jnp.float32
    hbm = pl.BlockSpec(memory_space=pltpu.HBM)
    dma = pltpu.SemaphoreType.DMA
    piece = (rows_dev, LANES)
    return pl.pallas_call(
        functools.partial(back_kernel, dims, block, rows_dev),
        out_shape=jax.ShapeDtypeStruct((rows_dev, columns), f32),
        in_specs=[pl.BlockSpec(memory_space=pltpu.SMEM)] + [hbm] * 4,
        out_specs=pl.BlockSpec(memory_space=pl.ANY),
        scratch_shapes=[
            pltpu.VMEM(gblk.shape, f32),
            pltpu.VMEM((block, block), f32),
            pltpu.VMEM((block, block), f32),
            pltpu.VMEM((chunks, ndp, nx) + piece, f32),
            [pltpu.VMEM((ndp, nx) + piece, f32) for _ in range(chunks)],
            pltpu.VMEM((chunks, nshard, CAP) + piece, f32),
            [pltpu.VMEM((nshard * CAP,) + piece, f32) for _ in range(chunks)],
            pltpu.VMEM((rows_dev, columns), f32),
            pltpu.VMEM((nbc, LANES), f32),
            pltpu.VMEM((ndp, nbc, LANES), f32),
            pltpu.VMEM((nbc, LANES), f32),
            pltpu.VMEM((nx, nbc, LANES), f32),
            dma((chunks, ndp)),
            dma((chunks, ndp)),
            dma((ndp,)),
            dma((ndp,)),
            dma((nx,)),
            dma((nx,)),
            dma((chunks, nshard)),
            dma((chunks, nshard)),
            dma((4,)),
        ],
        compiler_params=pltpu.CompilerParams(
            collective_id=1, has_side_effects=True, vmem_limit_bytes=53 * MIB),
    )(tab, gblk, lroot, rroot, adam)


def local(grad_parts, moment, second, left_prev, right_prev, owners, newton_steps):
    ndp = lax.axis_size("dp")
    nshard = lax.axis_size("shard")
    _, rows_dev, columns = moment.shape
    block = left_prev.shape[-1]
    nx = block // (rows_dev * ndp)
    dims = (ndp, nshard, nx, nshard // nx, columns // block)
    gblk, mom, sec, adam, tab = forward(
        owners[None], newton_steps[None], grad_parts[0], moment[0], second[0], dims, block)
    gblk = gblk.reshape(block // LANES, block, LANES)
    left, right, lroot, rroot, mom, sec = owner_step(
        tab, gblk, left_prev[0, 0, 0], right_prev[0, 0, 0], mom, sec, offsets(dims)[4])
    update = back(tab, gblk, lroot, rroot, adam, dims, block, rows_dev, columns)
    slots = (1, 1, 1, block, block)
    return (
        update[None],
        mom[None],
        sec[None],
        left.reshape(slots),
        right.reshape(slots),
        lroot.reshape(slots),
        rroot.reshape(slots),
    )


def solution(mesh):
    rows = P("shard", "dp", None)
    slots = P("dp", "shard", None, None, None)
    return jax.shard_map(
        local,
        mesh=mesh,
        in_specs=(P("dp", "shard", None), rows, rows, slots, slots, P(), P()),
        out_specs=(rows, rows, rows, slots, slots, slots, slots),
        check_vma=False,
    )
```

```python
import functools

import jax
import jax.numpy as jnp
from jax import lax
from jax.experimental import pallas as pl
from jax.experimental.pallas import tpu as pltpu
from jax.sharding import PartitionSpec as P

MESH = pl.DeviceIdType.MESH
CORES = 2
LANES = 128
CAP = 2
MIB = 1 << 20


def route_table(own, steps, my_dp, my_shard, dims):
    ndp, nshard, nx, nbr, nbc = dims
    count = nbr * nbc
    o_sends, o_rank, o_row, o_final, o_steps = offsets(dims)
    down = lax.broadcasted_iota(jnp.int32, (count, count), 0)
    across = lax.broadcasted_iota(jnp.int32, (count, count), 1)
    wide = jnp.broadcast_to(own, (count, count))

    def turned(row):
        return jnp.sum(jnp.where(down == across, jnp.broadcast_to(row, (count, count)), 0), axis=1, keepdims=True)

    owner = turned(own)
    earlier = jnp.where((owner == wide) & (across < down), 1, 0)
    rank = jnp.sum(earlier, axis=1, keepdims=True)
    sub = jnp.sum(jnp.where(across // nbc == down // nbc, earlier, 0), axis=1, keepdims=True)
    count_of = turned(steps)
    lane = lax.broadcasted_iota(jnp.int32, (count, 128), 1)
    block = lax.broadcasted_iota(jnp.int32, (count, 128), 0)

    def spread(column):
        return jnp.broadcast_to(column, (count, 128))

    owner, rank, sub, count_of = (spread(column) for column in (owner, rank, sub, count_of))
    row, column = block // nbc, block % nbc
    mine = jnp.where(owner == my_shard, 1, 0)
    here = jnp.where(row == my_shard // nx, 1, 0)
    slot = owner * CAP + sub
    place = row * CAP + sub
    key = jnp.where(lane < o_rank, slot, jnp.where(lane < o_row, rank + o_rank, jnp.where(
        lane < o_final, place + o_row, jnp.where(lane < o_steps, column + o_final, -1))))
    value = jnp.where(lane < o_rank, column, jnp.where(lane < o_row, place, jnp.where(
        lane < o_final, rank, slot)))
    chosen = jnp.where((lane < o_rank) | (lane >= o_final), here, mine)
    table = jnp.where(key == lane, value * chosen, 0)
    held = jnp.where(rank == my_dp, mine, 0)
    table = table + jnp.where(lane == o_steps, held * count_of, jnp.where(lane == o_steps + 1, held, 0))
    return jnp.sum(table, axis=0, keepdims=True)


def offsets(dims):
    ndp, nshard, nx, nbr, nbc = dims
    sends = 0
    by_rank = sends + nshard * CAP
    by_row = by_rank + ndp
    finals = by_row + nbr * CAP
    steps = finals + nbc
    return sends, by_rank, by_row, finals, steps


def signal(peers):
    barrier = pltpu.get_barrier_semaphore()
    for peer in peers:
        pl.semaphore_signal(barrier, inc=1, device_id=peer, device_id_type=MESH)


def await_peers(peers):
    pl.semaphore_wait(pltpu.get_barrier_semaphore(), len(peers))


def greet(peers):
    signal(peers)
    await_peers(peers)


def joined(chunked):
    return jnp.concatenate([chunked[t] for t in range(chunked.shape[0])], axis=1)


def far_first(count, width):
    def length(k):
        across, down = k % width, k // width
        high = count // width
        return min(across, width - across) + min(down, high - down)

    return sorted(range(1, count), key=lambda k: -length(k))


def dp_steps(ndp):
    nz = ndp // CORES
    steps = [(a, c) for a in range(nz) for c in range(CORES) if a or c]
    return sorted(steps, key=lambda k: -min(k[0], nz - k[0]))


def dp_peer(me_d, step, ndp):
    nz = ndp // CORES
    return (me_d // CORES + step[0]) % nz * CORES + (me_d % CORES + step[1]) % CORES


def early_blocks(nbc):
    return max(1, nbc // 8)


def forward_kernel(dims, block, own, steps, grad, mom, sec,
                   gblk, mom_out, sec_out, adam_out, tab_out,
                   ibuf, tvec, tab, loc, pair, raw, acc, first_up, first_down, from_below, from_above,
                   gsel, mbuf, vbuf, send1, recv1, send2, asend,
                   loc_sem, pair_s, pair_r, cross_s, cross_r, ring_s, ring_r, p1_s, p1_r, p2_s, p2_r,
                   io_sem, t_sem):
    ndp, nshard, nx, nbr, nbc = dims
    o_sends, o_rank, _, _, _ = offsets(dims)
    nz = ndp // CORES
    chunks = block // LANES
    half = nbc // 2
    rows_dev = mom.shape[0]
    me_d = lax.axis_index("dp")
    me_s = lax.axis_index("shard")
    z = me_d // CORES
    core = me_d % CORES

    def zed(step):
        return (z + step) % nz

    def rows_of(zz, cc):
        return pl.ds(pl.multiple_of((zz * CORES + cc) * rows_dev, rows_dev), rows_dev)

    order = (2, 1, nz - 1, 0)
    loads = []
    lists = [pltpu.make_async_copy(src, ibuf.at[i], t_sem.at[i]) for i, src in enumerate((own, steps))]
    for copy in lists:
        copy.start()
    for q, step in enumerate(order):
        loads.append(pltpu.make_async_copy(
            grad.at[rows_of(zed(step), core), :], loc.at[q], loc_sem.at[q]))
    loads[0].start()
    m_in = pltpu.make_async_copy(mom, mbuf, io_sem.at[0])
    v_in = pltpu.make_async_copy(sec, vbuf, io_sem.at[1])

    z_steps = dp_steps(ndp)
    s_steps = far_first(nshard, nx)
    greet([(dp_peer(me_d, step, ndp), me_s) for step in reversed(z_steps)]
          + [(me_d, shard_peer(me_s, k, dims)) for k in s_steps])

    sibling = (z * CORES + (1 - core), me_s)
    above = (zed(1) * CORES + core, me_s)
    below = (zed(nz - 1) * CORES + core, me_s)
    pairs = []
    for q, step in enumerate(order):
        pairs.append(pltpu.make_async_remote_copy(
            grad.at[rows_of(zed(step), 1 - core), :], pair.at[q],
            pair_s.at[q], pair_r.at[q], device_id=sibling, device_id_type=MESH))
    pairs[0].start()

    lo = pl.ds(0, half)
    hi = pl.ds(half, half)
    early = early_blocks(nbc)
    lo_rest = pl.ds(early, half - early)
    hi_rest = pl.ds(half + early, half - early)
    ring = {}
    cross = []

    def ring_send(t, index, src, dst, target):
        copy = pltpu.make_async_remote_copy(
            src, dst, ring_s.at[t, index], ring_r.at[t, index], device_id=target, device_id_type=MESH)
        copy.start()
        ring[t, index] = copy

    def merge(t, q):
        if t == 0:
            loads[q].wait()
            pairs[q].wait_recv()
        for c in range(nbc):
            cols = pl.ds(c * block + t * LANES, LANES)
            acc[t, q, c] = loc[q, :, cols] + pair[q, :, cols]

    def ring_raw():
        for index in range(4):
            side, swap = index // 2, index % 2
            target = (above, below)[side]
            copy = pltpu.make_async_remote_copy(
                grad.at[rows_of(zed(order[0]), (core + swap) % CORES), pl.ds(side * half * block, early * block)],
                raw.at[index], cross_s.at[index], cross_r.at[index],
                device_id=(target[0] + swap * (1 - 2 * core), me_s), device_id_type=MESH)
            copy.start()
            cross.append(copy)

    def ring_far(t):
        merge(t, 0)
        ring_send(t, 0, acc.at[t, 0, lo_rest], first_up.at[t], above)
        ring_send(t, 1, acc.at[t, 0, hi_rest], first_down.at[t], below)

    def add_raw(t, q, side):
        for c in range(early):
            cols = pl.ds(c * block + t * LANES, LANES)
            acc[t, q, side * half + c] = acc[t, q, side * half + c] + (
                raw[2 * side, :, cols] + raw[2 * side + 1, :, cols])

    def ring_one(t):
        merge(t, 1)
        ring_send(t, 2, acc.at[t, 1, hi], from_below.at[t, hi], above)
        merge(t, 2)
        ring_send(t, 3, acc.at[t, 2, lo], from_above.at[t, lo], below)
        merge(t, 3)

    def ring_two(t):
        ring[t, 0].wait_recv()
        if t == 0:
            for copy in cross:
                copy.wait_recv()
        add_raw(t, 1, 0)
        acc[t, 1, lo_rest] = acc[t, 1, lo_rest] + first_up[t]
        ring_send(t, 4, acc.at[t, 1, lo], from_below.at[t, lo], above)
        ring[t, 1].wait_recv()
        add_raw(t, 2, 1)
        acc[t, 2, hi_rest] = acc[t, 2, hi_rest] + first_down[t]
        ring_send(t, 5, acc.at[t, 2, hi], from_above.at[t, hi], below)

    def ring_end(t):
        for index in range(2, 6):
            ring[t, index].wait_recv()
        gsel[t] = (acc[t, 3] + from_below[t]) + from_above[t]

    p1 = {}

    def exchange_shards(t):
        for k in s_steps:
            target = shard_peer(me_s, k, dims)
            for j in range(CAP):
                send1[t, k, j] = gsel[t, tab[0, o_sends + target * CAP + j]]
            copy = pltpu.make_async_remote_copy(
                send1.at[t, k], recv1[t].at[me_s], p1_s.at[t, k], p1_r.at[t, k],
                device_id=(me_d, target), device_id_type=MESH)
            copy.start()
            p1[t, k] = copy
        for j in range(CAP):
            recv1[t][me_s, j] = gsel[t, tab[0, o_sends + me_s * CAP + j]]

    p2 = {}

    def exchange_dp(t):
        for k in s_steps:
            p1[t, k].wait_recv()
        for k, step in enumerate(z_steps + [(0, 0)]):
            target = dp_peer(me_d, step, ndp)
            place = tab[0, o_rank + target]
            r = place // CAP
            j = place % CAP
            for x in range(nx):
                send2[t, k, x] = recv1[t][r * nx + x, j]
            if k < len(z_steps):
                copy = pltpu.make_async_remote_copy(
                    send2.at[t, k], gblk.at[t, :, me_d], p2_s.at[t, k], p2_r.at[t, k],
                    device_id=(target, me_s), device_id_type=MESH)
            else:
                copy = pltpu.make_async_copy(send2.at[t, k], gblk.at[t, :, me_d], p2_s.at[t, k])
            copy.start()
            p2[t, k] = copy

    def adam_rows(t):
        for c in range(nbc):
            cols = pl.ds(c * block + t * LANES, LANES)
            g = gsel[t, c]
            m = 0.9 * mbuf[:, cols] + 0.1 * g
            v = 0.99 * vbuf[:, cols] + 0.01 * g * g
            mbuf[:, cols] = m
            vbuf[:, cols] = v
            a = m / (jnp.sqrt(v) + 1e-08)
            part = jnp.sum(a * a, axis=0, keepdims=True)
            if t == 0:
                asend[pl.ds(c, 1), :] = part
            else:
                asend[pl.ds(c, 1), :] = asend[pl.ds(c, 1), :] + part

    def shards_out(t):
        ring_end(t)
        exchange_shards(t)

    ring_raw()
    for load, copy in zip(loads[1:], pairs[1:]):
        load.start()
        copy.start()
    m_in.start()
    v_in.start()
    ring_far(0)
    ring_far(1)
    ring_one(0)
    for t in range(1, chunks):
        if t > 1:
            ring_far(t)
        ring_one(t)
        if t == 1:
            for copy in lists:
                copy.wait()
            tvec[...] = route_table(ibuf[0], ibuf[1], me_d, me_s, dims)
            table_in = pltpu.make_async_copy(tvec, tab, t_sem.at[0])
            table_in.start()
            table_out = pltpu.make_async_copy(tvec, tab_out, t_sem.at[1])
            table_out.start()
        ring_two(t - 1)
        if t == 1:
            table_in.wait()
        if t >= 2:
            shards_out(t - 2)
    ring_two(chunks - 1)
    m_in.wait()
    v_in.wait()
    sent = 0
    for t in range(max(chunks - 2, 0), chunks):
        if sent < t:
            exchange_dp(sent)
            sent += 1
        shards_out(t)
    done = 0
    while sent < chunks:
        if sent < chunks - 2:
            exchange_dp(sent)
            sent += 1
        for _ in range(2):
            if done < chunks:
                adam_rows(done)
                done += 1
        exchange_dp(sent)
        sent += 1
    while done < chunks:
        adam_rows(done)
        done += 1

    m_out = pltpu.make_async_copy(mbuf, mom_out, io_sem.at[0])
    v_out = pltpu.make_async_copy(vbuf, sec_out, io_sem.at[1])
    a_out = pltpu.make_async_copy(asend, adam_out, io_sem.at[2])
    for copy in (m_out, v_out, a_out):
        copy.start()

    for copy in pairs + cross + list(ring.values()) + list(p1.values()):
        copy.wait_send()
    for (t, k), copy in p2.items():
        if k < len(z_steps):
            copy.wait_send()
            copy.wait_recv()
        else:
            copy.wait()
    m_out.wait()
    v_out.wait()
    a_out.wait()
    table_out.wait()


def shard_peer(me_s, k, dims):
    _, _, nx, nbr, _ = dims
    return (me_s // nx + k // nx) % nbr * nx + (me_s % nx + k % nx) % nx


def forward(own, steps, grad, mom, sec, dims, block):
    ndp, nshard, nx, nbr, nbc = dims
    rows_dev, columns = mom.shape
    chunks = block // LANES
    f32 = jnp.float32
    hbm = pl.BlockSpec(memory_space=pltpu.HBM)
    dma = pltpu.SemaphoreType.DMA
    piece = (rows_dev, LANES)
    return pl.pallas_call(
        functools.partial(forward_kernel, dims, block),
        out_shape=(
            jax.ShapeDtypeStruct((chunks, nx, ndp) + piece, f32),
            jax.ShapeDtypeStruct((rows_dev, columns), f32),
            jax.ShapeDtypeStruct((rows_dev, columns), f32),
            jax.ShapeDtypeStruct((nbc, LANES), f32),
            jax.ShapeDtypeStruct((1, LANES), jnp.int32),
        ),
        in_specs=[hbm] * 5,
        out_specs=(hbm,) * 5,
        scratch_shapes=[
            pltpu.VMEM((2, 1, nbr * nbc), jnp.int32),
            pltpu.VMEM((1, LANES), jnp.int32),
            pltpu.SMEM((1, LANES), jnp.int32),
            pltpu.VMEM((4, rows_dev, columns), f32),
            pltpu.VMEM((4, rows_dev, columns), f32),
            pltpu.VMEM((4, rows_dev, early_blocks(nbc) * block), f32),
            pltpu.VMEM((chunks, 4, nbc) + piece, f32),
            pltpu.VMEM((chunks, nbc // 2 - early_blocks(nbc)) + piece, f32),
            pltpu.VMEM((chunks, nbc // 2 - early_blocks(nbc)) + piece, f32),
            pltpu.VMEM((chunks, nbc) + piece, f32),
            pltpu.VMEM((chunks, nbc) + piece, f32),
            pltpu.VMEM((chunks, nbc) + piece, f32),
            pltpu.VMEM((rows_dev, columns), f32),
            pltpu.VMEM((rows_dev, columns), f32),
            pltpu.VMEM((chunks, nshard, CAP) + piece, f32),
            [pltpu.VMEM((nshard, CAP) + piece, f32) for _ in range(chunks)],
            pltpu.VMEM((chunks, ndp, nx) + piece, f32),
            pltpu.VMEM((nbc, LANES), f32),
            dma((4,)),
            dma((4,)),
            dma((4,)),
            dma((4,)),
            dma((4,)),
            dma((chunks, 6)),
            dma((chunks, 6)),
            dma((chunks, nshard)),
            dma((chunks, nshard)),
            dma((chunks, ndp)),
            dma((chunks, ndp)),
            dma((3,)),
            dma((2,)),
        ],
        compiler_params=pltpu.CompilerParams(
            collective_id=0, has_side_effects=True, vmem_limit_bytes=58 * MIB),
    )(own, steps, grad, mom, sec)


def split(value):
    high = value.astype(jnp.bfloat16)
    low = (value - high.astype(jnp.float32)).astype(jnp.bfloat16)
    return high, low


def dot(left, right, axes=((1,), (0,))):
    return lax.dot_general(left, right, (axes, ((), ())), preferred_element_type=jnp.float32)


def product(first, second_factor):
    return dot(first[0], second_factor[0]) + (
        dot(first[0], second_factor[1]) + dot(first[1], second_factor[0]))


def mirrored(top, corner):
    half = corner.shape[0]
    return jnp.concatenate([top, jnp.concatenate([top[:, half:].T, corner], axis=1)], axis=0)


def gram(value, axes):
    cross = dot(value[0], value[1], axes)
    return dot(value[0], value[0], axes) + (cross + cross.T)


def square_of(value):
    high, low = value
    half = high.shape[0] // 2
    cross = dot(high, low)
    top = dot(high[:half], high) + (
        cross[:half] + jnp.concatenate([cross[:half, :half].T, cross[half:, :half].T], axis=1))
    corner = dot(high[half:], high[:, half:]) + (cross[half:, half:] + cross[half:, half:].T)
    return mirrored(top, corner)


def even_product(first, second_factor):
    half = first[0].shape[0] // 2
    top = product((first[0][:half], first[1][:half]), second_factor)
    corner = product(
        (first[0][half:], first[1][half:]), (second_factor[0][:, half:], second_factor[1][:, half:]))
    return mirrored(top, corner)


def owner_kernel(step_place, tab, gblk, left_prev, right_prev, mom, sec,
                 left_out, right_out, lroot_out, rroot_out, mom_out, sec_out,
                 g_ref, stat, root, mbuf, vbuf, sem, io_sem):
    taken = tab[0, step_place + 1]
    size = g_ref.shape[1]
    g_in = pltpu.make_async_copy(gblk, g_ref, sem.at[0])
    ins = [pltpu.make_async_copy(prev, stat.at[i], sem.at[1 + i])
           for i, prev in enumerate((left_prev, right_prev))]
    g_in.start()
    for copy in ins:
        copy.start()
    moves = [pltpu.make_async_copy(src, dst, io_sem.at[i])
             for i, (src, dst) in enumerate(((mom, mbuf), (sec, vbuf)))]
    for copy in moves:
        copy.start()
    g_in.wait()
    for copy in ins:
        copy.wait()
    for copy in moves:
        copy.wait()
    moves = [pltpu.make_async_copy(src, dst, io_sem.at[i])
             for i, (src, dst) in enumerate(((mbuf, mom_out), (vbuf, sec_out)))]
    for copy in moves:
        copy.start()
    stat_outs = [pltpu.make_async_copy(stat.at[i], out, sem.at[1 + i])
                 for i, out in enumerate((left_out, right_out))]
    root_outs = [pltpu.make_async_copy(root.at[i], out, sem.at[3 + i])
                 for i, out in enumerate((lroot_out, rroot_out))]
    two = range(2)

    @pl.when(taken == 0)
    def _():
        for i in two:
            stat[i] = jnp.zeros((size, size), jnp.float32)
            root[i] = jnp.zeros((size, size), jnp.float32)
            stat_outs[i].start()
            root_outs[i].start()
        for i in two:
            stat_outs[i].wait()
            root_outs[i].wait()

    @pl.when(taken != 0)
    def _():
        diagonal = lax.broadcasted_iota(jnp.int32, (size, size), 0) == lax.broadcasted_iota(
            jnp.int32, (size, size), 1)

        def complement(matrix):
            return split(jnp.where(diagonal, 1.25, 0.0) - 0.25 * matrix)

        g = split(joined(g_ref))
        grams = [gram(g, axes) for axes in (((1,), (1,)), ((0,), (0,)))]
        for i in two:
            stat[i] = 0.95 * stat[i] + grams[i]
            stat_outs[i].start()
        scales, matrix = [], []
        for i in two:
            shifted = stat[i] + jnp.where(diagonal, 0.0001, 0.0)
            scale = 2.5 / jnp.sqrt(jnp.full((1, 1), jnp.sum(shifted * shifted)))
            scales.append(jnp.sqrt(jnp.sqrt(scale)))
            matrix.append(scale * shifted)
        factor = [complement(matrix[i]) for i in two]
        square = [split(square_of(factor[i])) for i in two]
        fourth = [split(square_of(square[i])) for i in two]
        matrix = [even_product(fourth[i], split(matrix[i])) for i in two]
        after = [complement(matrix[i]) for i in two]
        square = [split(square_of(after[i])) for i in two]
        current = [even_product(factor[i], after[i]) for i in two]
        fourth = [split(square_of(square[i])) for i in two]
        matrix = [even_product(fourth[i], split(matrix[i])) for i in two]
        more = tab[0, step_place] > 2
        for i in two:
            third = even_product(split(current[i]), complement(matrix[i]))
            root[i] = scales[i] * jnp.where(more, third, current[i])
            root_outs[i].start()
        for i in two:
            stat_outs[i].wait()
            root_outs[i].wait()

    for copy in moves:
        copy.wait()


def owner_step(tab, gblk, left_prev, right_prev, mom, sec, step_place):
    size = gblk.shape[1]
    f32 = jnp.float32
    square = jax.ShapeDtypeStruct((size, size), f32)
    rows = jax.ShapeDtypeStruct(mom.shape, f32)
    hbm = pl.BlockSpec(memory_space=pltpu.HBM)
    return pl.pallas_call(
        functools.partial(owner_kernel, step_place),
        out_shape=(square,) * 4 + (rows,) * 2,
        in_specs=[pl.BlockSpec(memory_space=pltpu.SMEM)] + [hbm] * 5,
        out_specs=(hbm,) * 6,
        scratch_shapes=[
            pltpu.VMEM(gblk.shape, f32),
            pltpu.VMEM((2, size, size), f32),
            pltpu.VMEM((2, size, size), f32),
            pltpu.VMEM(mom.shape, f32),
            pltpu.VMEM(mom.shape, f32),
            pltpu.SemaphoreType.DMA((5,)),
            pltpu.SemaphoreType.DMA((2,)),
        ],
        compiler_params=pltpu.CompilerParams(vmem_limit_bytes=58 * MIB),
        cost_estimate=pl.CostEstimate(
            flops=100 * size ** 3, bytes_accessed=36 * size * size, transcendentals=0),
    )(tab, gblk, left_prev, right_prev, mom, sec)


def back_kernel(dims, block, rows_dev, tab, gblk, lroot, rroot, adam, update,
                gbuf, lbuf, rbuf, pbuf, recv2, send1, recv1, out, asend, arecv, xsend, xrecv,
                p2_s, p2_r, a_s, a_r, x_s, x_r, p1_s, p1_r, io_sem):
    ndp, nshard, nx, nbr, nbc = dims
    _, _, o_row, o_final, _ = offsets(dims)
    chunks = block // LANES
    me_d = lax.axis_index("dp")
    me_s = lax.axis_index("shard")
    ins = [pltpu.make_async_copy(src, dst, io_sem.at[i])
           for i, (src, dst) in enumerate(((lroot, lbuf), (gblk, gbuf), (rroot, rbuf), (adam, asend)))]
    for copy in ins:
        copy.start()
    z_steps = dp_steps(ndp)
    s_steps = far_first(nshard, nx)
    peers = [(dp_peer(me_d, step, ndp), me_s) for step in z_steps] + [
        (me_d, shard_peer(me_s, k, dims)) for k in s_steps]
    signal(peers)
    for copy in ins:
        copy.wait()
    turned = split(product(split(lbuf[...]), split(joined(gbuf))))
    way = product(turned, split(rbuf[...]))
    power = jnp.sum(jnp.sum(way * way, axis=0, keepdims=True), axis=1, keepdims=True)
    way = way * (1.0 / jnp.sqrt(power + 1e-12))
    for t in range(chunks):
        for x in range(nx):
            for d in range(ndp):
                top = (x * ndp + d) * rows_dev
                pbuf[t, d, x] = way[top:top + rows_dev, t * LANES:(t + 1) * LANES]
    await_peers(peers)

    acopies = []
    for k, step in enumerate(z_steps):
        copy = pltpu.make_async_remote_copy(
            asend, arecv.at[k], a_s.at[k], a_r.at[k],
            device_id=(dp_peer(me_d, step, ndp), me_s), device_id_type=MESH)
        copy.start()
        acopies.append(copy)
    p2 = {}
    for t in range(chunks):
        for k, step in enumerate(z_steps):
            target = dp_peer(me_d, step, ndp)
            copy = pltpu.make_async_remote_copy(
                pbuf.at[t, target], recv2[t].at[me_d], p2_s.at[t, k], p2_r.at[t, k],
                device_id=(target, me_s), device_id_type=MESH)
            copy.start()
            p2[t, k] = copy
        recv2[t][me_d] = pbuf[t, me_d]
    total = asend[...]
    for k, copy in enumerate(acopies):
        copy.wait_recv()
        total = total + arecv[k]
    xsend[...] = total
    xcopies = []
    for k in range(1, nx):
        copy = pltpu.make_async_remote_copy(
            xsend, xrecv.at[k], x_s.at[k], x_r.at[k],
            device_id=(me_d, me_s // nx * nx + (me_s % nx + k) % nx), device_id_type=MESH)
        copy.start()
        xcopies.append(copy)

    p1 = {}
    for t in range(chunks):
        for k in range(len(z_steps)):
            p2[t, k].wait_recv()

        def wanted(target, j):
            rank = tab[0, o_row + target // nx * CAP + j]
            return recv2[t][rank, target % nx]

        for k in s_steps:
            target = shard_peer(me_s, k, dims)
            for j in range(CAP):
                send1[t, k, j] = wanted(target, j)
            copy = pltpu.make_async_remote_copy(
                send1.at[t, k], recv1[t].at[pl.ds(me_s * CAP, CAP)], p1_s.at[t, k], p1_r.at[t, k],
                device_id=(me_d, target), device_id_type=MESH)
            copy.start()
            p1[t, k] = copy
        for j in range(CAP):
            recv1[t][me_s * CAP + j] = wanted(me_s, j)
    for k in range(1, nx):
        xcopies[k - 1].wait_recv()
        total = total + xrecv[k]
    ad = jnp.broadcast_to(jnp.sqrt(jnp.sum(total, axis=1, keepdims=True)), total.shape)
    for t in range(chunks):
        for k in s_steps:
            p1[t, k].wait_recv()
        for c in range(nbc):
            cols = pl.ds(c * block + t * LANES, LANES)
            update[:, cols] = recv1[t][tab[0, o_final + c]] * ad[c:c + 1, :]
    for copy in list(p2.values()) + acopies + xcopies + list(p1.values()):
        copy.wait_send()


def back(tab, gblk, lroot, rroot, adam, dims, block, rows_dev, columns):
    ndp, nshard, nx, nbr, nbc = dims
    chunks = block // LANES
    f32 = jnp.float32
    hbm = pl.BlockSpec(memory_space=pltpu.HBM)
    dma = pltpu.SemaphoreType.DMA
    piece = (rows_dev, LANES)
    return pl.pallas_call(
        functools.partial(back_kernel, dims, block, rows_dev),
        out_shape=jax.ShapeDtypeStruct((rows_dev, columns), f32),
        in_specs=[pl.BlockSpec(memory_space=pltpu.SMEM)] + [hbm] * 4,
        out_specs=pl.BlockSpec(memory_space=pltpu.VMEM),
        scratch_shapes=[
            pltpu.VMEM(gblk.shape, f32),
            pltpu.VMEM((block, block), f32),
            pltpu.VMEM((block, block), f32),
            pltpu.VMEM((chunks, ndp, nx) + piece, f32),
            [pltpu.VMEM((ndp, nx) + piece, f32) for _ in range(chunks)],
            pltpu.VMEM((chunks, nshard, CAP) + piece, f32),
            [pltpu.VMEM((nshard * CAP,) + piece, f32) for _ in range(chunks)],
            pltpu.VMEM((rows_dev, columns), f32),
            pltpu.VMEM((nbc, LANES), f32),
            pltpu.VMEM((ndp, nbc, LANES), f32),
            pltpu.VMEM((nbc, LANES), f32),
            pltpu.VMEM((nx, nbc, LANES), f32),
            dma((chunks, ndp)),
            dma((chunks, ndp)),
            dma((ndp,)),
            dma((ndp,)),
            dma((nx,)),
            dma((nx,)),
            dma((chunks, nshard)),
            dma((chunks, nshard)),
            dma((4,)),
        ],
        compiler_params=pltpu.CompilerParams(
            collective_id=1, has_side_effects=True, vmem_limit_bytes=53 * MIB),
    )(tab, gblk, lroot, rroot, adam)


def local(grad_parts, moment, second, left_prev, right_prev, owners, newton_steps):
    ndp = lax.axis_size("dp")
    nshard = lax.axis_size("shard")
    _, rows_dev, columns = moment.shape
    block = left_prev.shape[-1]
    nx = block // (rows_dev * ndp)
    dims = (ndp, nshard, nx, nshard // nx, columns // block)
    gblk, mom, sec, adam, tab = forward(
        owners[None], newton_steps[None], grad_parts[0], moment[0], second[0], dims, block)
    gblk = gblk.reshape(block // LANES, block, LANES)
    left, right, lroot, rroot, mom, sec = owner_step(
        tab, gblk, left_prev[0, 0, 0], right_prev[0, 0, 0], mom, sec, offsets(dims)[4])
    update = back(tab, gblk, lroot, rroot, adam, dims, block, rows_dev, columns)
    slots = (1, 1, 1, block, block)
    return (
        update[None],
        mom[None],
        sec[None],
        left.reshape(slots),
        right.reshape(slots),
        lroot.reshape(slots),
        rroot.reshape(slots),
    )


def solution(mesh):
    rows = P("shard", "dp", None)
    slots = P("dp", "shard", None, None, None)
    return jax.shard_map(
        local,
        mesh=mesh,
        in_specs=(P("dp", "shard", None), rows, rows, slots, slots, P(), P()),
        out_specs=(rows, rows, rows, slots, slots, slots, slots),
        check_vma=False,
    )
```
